128 devices in a mesh: seq: 32 (over x, y, core), batch: 4 (over z).
Axes of the slice: x: 4, y: 4, z: 4, core: 2. Of those that a mesh axis runs over, the one named last changes fastest.
Arguments:
- tokens: bfloat16 [4, 16384, 2048], P('batch', 'seq'), may hold values from -6 to 6
- w_qkv: bfloat16 [2048, 3072], replicated, may hold values from -0.125 to 0.125
- cotangent: bfloat16 [4, 16384, 1024], P('batch', 'seq'), may hold values from -6 to 6
Outputs:
- attended: bfloat16 [4, 16384, 1024], P('batch', 'seq')
- token_grad: bfloat16 [4, 16384, 2048], P('batch', 'seq')
- weight_grad: float32 [2048, 3072], P('seq')
The draws below stay inside these ranges and needn't reach their ends.
All inputs are finite; a program needn't handle non-finite values.
Results may differ from the reference program's by a relative error of at most 0.0064.
Values sent between devices are 32-bit elements; how exact they have to be, the bound alone decides.
No kernel may reach another device: no remote copies, remote signals or barrier semaphores. Data moves between devices by JAX's collectives and lax.ppermute only.
A program may use at most 192 MiB of HBM per device.

```python
import jax
import jax.numpy as jnp
from jax import lax

D = 2048
HEADS = 8
DH = 128
BLK = 512
HD = 1024
SEQS = 4
LENGTH = 16384


def block_scale(rng, dims, pieces, low, high):
    level, own = 1.0, jax.random.fold_in(rng, 6)
    for dim, blocks in pieces:
        draws = jnp.exp(jax.random.uniform(jax.random.fold_in(own, dim), (blocks,), jnp.float32, low / len(pieces), high / len(pieces)))
        level = level * jnp.repeat(draws, dims[dim] // blocks).reshape([-1 if axis == dim else 1 for axis in range(len(dims))])
    return level


def bell_draw(rng, shape, spread, reach, split=(), dtype=jnp.bfloat16):
    array = spread * jax.random.normal(rng, shape, jnp.float32)
    if split:
        array = array * block_scale(rng, shape, split, -0.22, 0.18)
    return jnp.clip(array, -reach, reach).astype(dtype)


def setup_inputs(seed: int = 0) -> dict:
    keys = jax.random.split(jax.random.key(seed), 4)
    tokens = bell_draw(keys[0], (SEQS, LENGTH, D), 1.0, 6.0, ((0, 4), (1, 32)))
    w_qkv = bell_draw(keys[1], (D, 3 * HD), D ** -0.5, 0.125)
    cotangent = bell_draw(keys[2], (SEQS, LENGTH, HD), 1.0, 6.0, ((0, 4), (1, 32)))
    return dict(tokens=tokens, w_qkv=w_qkv, cotangent=cotangent)


PRECISE = lax.Precision.HIGHEST

def exclusive_running(block_states, reverse):
    zero_block = jnp.zeros_like(block_states[:1])
    if reverse:
        totals = jnp.cumsum(block_states[::-1], axis=0)[::-1]
        return jnp.concatenate([totals[1:], zero_block], 0)
    totals = jnp.cumsum(block_states, axis=0)
    return jnp.concatenate([zero_block, totals[:-1]], 0)

def rounded(value):
    low = lax.optimization_barrier(value.astype(jnp.bfloat16))
    return low.astype(jnp.float32)

def one_sequence(seq_tokens, w_qkv, seq_cotangent):
    length = seq_tokens.shape[0]
    width = w_qkv.shape[1] // 3
    block_count = length // BLK
    projected = jnp.dot(seq_tokens, w_qkv, preferred_element_type=jnp.float32).astype(jnp.bfloat16)

    def to_heads(block):
        return block.reshape(block_count, BLK, HEADS, DH).astype(jnp.float32)
    queries = to_heads(projected[:, :width])
    key_heads = to_heads(projected[:, width:2 * width])
    value_heads = to_heads(projected[:, 2 * width:])
    position = jnp.arange(length).astype(jnp.float32)
    pos_scale = DH ** (-0.5) / jnp.sqrt(position + 1.0)
    scaled_grad = (seq_cotangent.astype(jnp.float32) * pos_scale[:, None]).astype(jnp.bfloat16)
    grad_heads = to_heads(scaled_grad)
    kv_blocks = jnp.einsum('nrha,nrhb->nhab', key_heads, value_heads, precision=PRECISE)
    grad_blocks = jnp.einsum('nrha,nrhb->nhab', queries, grad_heads, precision=PRECISE)
    kv_before = exclusive_running(kv_blocks, False)
    grad_after = exclusive_running(grad_blocks, True)
    causal = jnp.arange(BLK)[:, None] >= jnp.arange(BLK)[None, :]
    scale_blocks = pos_scale.reshape(block_count, BLK)

    def one_block(block_items):
        query, key_part, value_part, grad_part, kv_state, grad_state, scale_part = block_items
        scores = rounded(jnp.where(causal, jnp.einsum('ihd,jhd->hij', query, key_part, precision=PRECISE), 0.0))
        grad_scores = rounded(jnp.where(causal, jnp.einsum('ihd,jhd->hij', grad_part, value_part, precision=PRECISE), 0.0))
        attended = jnp.einsum('hij,jhd->ihd', scores, value_part, precision=PRECISE)
        attended = (attended + jnp.einsum('ihd,hde->ihe', query, kv_state, precision=PRECISE)) * scale_part[:, None, None]
        query_grad = jnp.einsum('hij,jhd->ihd', grad_scores, key_part, precision=PRECISE)
        query_grad = query_grad + jnp.einsum('ihe,hde->ihd', grad_part, kv_state, precision=PRECISE)
        key_grad = jnp.einsum('hij,ihd->jhd', grad_scores, query, precision=PRECISE)
        key_grad = key_grad + jnp.einsum('jhe,hde->jhd', value_part, grad_state, precision=PRECISE)
        value_grad = jnp.einsum('hij,ihe->jhe', scores, grad_part, precision=PRECISE)
        value_grad = value_grad + jnp.einsum('jhd,hde->jhe', key_part, grad_state, precision=PRECISE)
        return (attended.astype(jnp.bfloat16), query_grad.astype(jnp.bfloat16), key_grad.astype(jnp.bfloat16), value_grad.astype(jnp.bfloat16))
    results = lax.map(one_block, (queries, key_heads, value_heads, grad_heads, kv_before, grad_after, scale_blocks))
    attended = results[0].reshape(length, width)
    qkv_grad = jnp.concatenate([results[1].reshape(length, width), results[2].reshape(length, width), results[3].reshape(length, width)], 1)
    token_grad = jnp.dot(qkv_grad, w_qkv.T, preferred_element_type=jnp.float32).astype(jnp.bfloat16)
    weight_part = jnp.dot(seq_tokens.T, qkv_grad, preferred_element_type=jnp.float32)
    return (attended, token_grad, weight_part)

def reference(tokens, w_qkv, cotangent):
    seq_total = tokens.shape[0]
    length = tokens.shape[1]
    attended_list = []
    token_list = []
    weight_sum = jnp.zeros(w_qkv.shape, jnp.float32)
    for number in range(seq_total):
        attended, token_grad, weight_part = one_sequence(tokens[number], w_qkv, cotangent[number])
        attended_list.append(attended)
        token_list.append(token_grad)
        weight_sum = weight_sum + weight_part
    weight_grad = weight_sum / jnp.sqrt(jnp.float32(seq_total * length))
    return (jnp.stack(attended_list, 0), jnp.stack(token_list, 0), weight_grad)
```

```python
import functools

import jax
import jax.numpy as jnp
from jax import lax
from jax.experimental import pallas as pl
from jax.experimental.pallas import tpu as pltpu
from jax.sharding import PartitionSpec as P

HEADS = 8
DH = 128
BLK = 512
D = 2048
HALF = 512
NEAR = 4
F32 = jnp.float32
BF16 = jnp.bfloat16
AXES = ("seq", "batch")
VMEM = 40 * 1024 * 1024


def flat(x, y, c, z):
    return ((x * 4 + y) * 2 + c) * 4 + z


def every():
    for x in range(4):
        for y in range(4):
            for c in range(2):
                for z in range(4):
                    yield x, y, c, z


def shift_pairs(axis, d):
    pairs = []
    for x, y, c, z in every():
        to = dict(x=x, y=y, z=z)
        to[axis] = (to[axis] + d) % 4
        pairs.append((flat(x, y, c, z), flat(to["x"], to["y"], c, to["z"])))
    return pairs


def core_pairs():
    return [(flat(x, y, c, z), flat(x, y, 1 - c, z)) for x, y, c, z in every()]


def partner(v, kind):
    return jnp.where(kind == 0, v ^ 1, 3 - v)


def halving_pairs(axis, step):
    pairs = []
    for x, y, c, z in every():
        to = dict(x=x, y=y, z=z)
        v = to[axis]
        to[axis] = v ^ 1 if (c + step) % 2 == 0 else 3 - v
        pairs.append((flat(x, y, c, z), flat(to["x"], to["y"], c, to["z"])))
    return pairs


def permute(value, pairs):
    return lax.ppermute(value, AXES, pairs)


def params():
    return pltpu.CompilerParams(vmem_limit_bytes=VMEM)


def cost(flops, moved):
    return pl.CostEstimate(flops=flops, bytes_accessed=moved, transcendentals=0)


def dot(a, b, contract_a, contract_b):
    return lax.dot_general(
        a, b, (((contract_a,), (contract_b,)), ((), ())), preferred_element_type=F32
    )


def project_kernel(core, x_ref, w_ref, o_ref):
    del core
    o_ref[...] = dot(x_ref[...], w_ref[...], 1, 0).astype(BF16)


def project_wide_kernel(core, x_ref, w_ref, o_ref, low_ref):
    del core

    @pl.when(pl.program_id(0) == 0)
    def _():
        low_ref[...] = x_ref[...].astype(BF16)

    o_ref[...] = dot(low_ref[...], w_ref[...], 1, 0).astype(BF16)


def project(x, w, core):
    wide = x.dtype == F32
    cols = 256
    per = HALF // cols
    out_shape = [jax.ShapeDtypeStruct((BLK, 3 * HALF), BF16)]
    out_specs = [pl.BlockSpec((BLK, cols), lambda j, c: (0, j))]
    if wide:
        out_shape.append(jax.ShapeDtypeStruct((BLK, D), BF16))
        out_specs.append(pl.BlockSpec((BLK, D), lambda j, c: (0, 0)))
    return pl.pallas_call(
        project_wide_kernel if wide else project_kernel,
        out_shape=out_shape,
        grid_spec=pltpu.PrefetchScalarGridSpec(
            num_scalar_prefetch=1,
            grid=(3 * per,),
            in_specs=[
                pl.BlockSpec((BLK, D), lambda j, c: (0, 0)),
                pl.BlockSpec((D, cols), lambda j, c: (0, (j // per) * 2 * per + c[0] * per + j % per)),
            ],
            out_specs=out_specs,
        ),
        compiler_params=params(),
        cost_estimate=cost(2 * BLK * D * 3 * HALF, 12 << 20),
        name="project",
    )(core, x, w)


def state_kernel(q_ref, k_ref, v_ref, g_ref, st_ref, low_ref):
    low = g_ref[...].astype(BF16)
    low_ref[...] = low
    st_ref[0, 0] = dot(k_ref[...], v_ref[...], 0, 0)
    st_ref[0, 1] = dot(q_ref[...], low, 0, 0)


def head_spec(kind):
    return pl.BlockSpec((BLK, DH), lambda h: (0, kind * NEAR + h))


def states(proj, grad):
    return pl.pallas_call(
        state_kernel,
        out_shape=[
            jax.ShapeDtypeStruct((NEAR, 2, DH, DH), F32),
            jax.ShapeDtypeStruct((BLK, HALF), BF16),
        ],
        grid=(NEAR,),
        in_specs=[head_spec(0), head_spec(1), head_spec(2), head_spec(0)],
        out_specs=[pl.BlockSpec((1, 2, DH, DH), lambda h: (h, 0, 0, 0)), head_spec(0)],
        compiler_params=params(),
        cost_estimate=cost(4 * BLK * DH * HALF, 4 << 20),
        name="states",
    )(proj, proj, proj, grad)


def intra_kernel(q_ref, k_ref, v_ref, g_ref, att_ref, dq_ref, dk_ref, dv_ref):
    q, k, v, g = q_ref[...], k_ref[...], v_ref[...], g_ref[...]
    rows = lax.broadcasted_iota(jnp.int32, (BLK, BLK), 0)
    cols = lax.broadcasted_iota(jnp.int32, (BLK, BLK), 1)
    causal = rows >= cols
    scores = jnp.where(causal, dot(q, k, 1, 1), 0.0).astype(BF16)
    att_ref[...] = dot(scores, v, 1, 0)
    dv_ref[...] = dot(scores, g, 0, 0)
    grad_scores = jnp.where(causal, dot(g, v, 1, 1), 0.0).astype(BF16)
    dq_ref[...] = dot(grad_scores, k, 1, 0)
    dk_ref[...] = dot(grad_scores, q, 0, 0)


def intra(proj, low):
    return pl.pallas_call(
        intra_kernel,
        out_shape=[jax.ShapeDtypeStruct((BLK, HALF), F32)] * 4,
        grid=(NEAR,),
        in_specs=[head_spec(0), head_spec(1), head_spec(2), head_spec(0)],
        out_specs=[head_spec(0)] * 4,
        compiler_params=params(),
        cost_estimate=cost(12 * BLK * BLK * HALF, 6 << 20),
        name="intra",
    )(proj, proj, proj, low)


def inter_kernel(
    where, q_ref, k_ref, v_ref, g_ref, att_ref, dq_ref, dk_ref, dv_ref, st_ref,
    oatt_ref, odq_ref, odk_ref, odv_ref,
):
    kv = st_ref[0, 0].astype(BF16)
    gr = st_ref[0, 1].astype(BF16)
    position = where[1] + lax.broadcasted_iota(jnp.int32, (BLK, DH), 0)
    scale = DH ** (-0.5) / jnp.sqrt(position.astype(F32) + 1.0)
    g = g_ref[...]
    att = att_ref[...] + dot(q_ref[...], kv, 1, 0)
    oatt_ref[...] = (att * scale).astype(BF16) if oatt_ref.dtype == BF16 else att
    odq_ref[...] = (dq_ref[...] + dot(g, kv, 1, 1)).astype(BF16)
    odk_ref[...] = (dk_ref[...] + dot(v_ref[...], gr, 1, 1)).astype(BF16)
    odv_ref[...] = (dv_ref[...] + dot(k_ref[...], gr, 1, 0)).astype(BF16)


def inter(proj, low, parts, state, where, out_type):
    def at(kind):
        return pl.BlockSpec((BLK, DH), lambda j, w: (0, kind * NEAR + (w[0] - j + 4) % 4))

    return pl.pallas_call(
        inter_kernel,
        out_shape=[jax.ShapeDtypeStruct((BLK, HALF), out_type)]
        + [jax.ShapeDtypeStruct((BLK, HALF), BF16)] * 3,
        grid_spec=pltpu.PrefetchScalarGridSpec(
            num_scalar_prefetch=1,
            grid=(NEAR,),
            in_specs=[at(0), at(1), at(2), at(0)]
            + [at(0)] * 4
            + [pl.BlockSpec((1, 2, DH, DH), lambda j, w: (j, 0, 0, 0))],
            out_specs=[at(0)] * 4,
        ),
        compiler_params=params(),
        cost_estimate=cost(8 * BLK * DH * HALF, 10 << 20),
        name="inter",
    )(where, proj, proj, proj, low, *parts, state)


def turn_kernel(x_ref, o_ref):
    o_ref[...] = x_ref[...].T


def turned(value):
    return pl.pallas_call(
        turn_kernel,
        out_shape=jax.ShapeDtypeStruct((D, BLK), BF16),
        grid=(4,),
        in_specs=[pl.BlockSpec((BLK, 512), lambda j: (0, j))],
        out_specs=pl.BlockSpec((512, BLK), lambda j: (j, 0)),
        compiler_params=params(),
        cost_estimate=cost(0, 4 << 20),
        name="turned",
    )(value)


def rows_kernel(pick, xo_ref, xp_ref, do_ref, dp_ref, o_ref):
    del pick
    for y in range(4):
        at = pl.ds(y * 128, 128)
        total = dot(xo_ref[at, :], do_ref[...], 1, 0) + dot(xp_ref[at, :], dp_ref[...], 1, 0)
        for z in range(4):
            o_ref[0, y, z] = total[:, z * 128 : (z + 1) * 128]


def partial_x(xo, xp, do, dp, pick):
    left = pl.BlockSpec((512, BLK), lambda g, p: (p[g], 0))
    right = pl.BlockSpec((BLK, HALF), lambda g, p: (0, 0))
    return pl.pallas_call(
        rows_kernel,
        out_shape=jax.ShapeDtypeStruct((2, 4, 4, 128, 128), F32),
        grid_spec=pltpu.PrefetchScalarGridSpec(
            num_scalar_prefetch=1,
            grid=(2,),
            in_specs=[left, left, right, right],
            out_specs=pl.BlockSpec((1, 4, 4, 128, 128), lambda g, p: (g, 0, 0, 0, 0)),
        ),
        compiler_params=params(),
        cost_estimate=cost(2 * 1024 * 1024 * 512, 6 << 20),
        name="partial_x",
    )(pick, xo, xp, do, dp)


def short_kernel(pick, xo_ref, xp_ref, do_ref, dp_ref, o_ref):
    del pick
    total = dot(xo_ref[...], do_ref[...], 1, 0) + dot(xp_ref[...], dp_ref[...], 1, 0)
    for z in range(4):
        o_ref[0, z, 0] = total[:, z * 128 : (z + 1) * 128]


def partial_y(xo, xp, do, dp, pick):
    left = pl.BlockSpec((128, BLK), lambda g, x, p: (x * 4 + p[g], 0))
    right = pl.BlockSpec((BLK, HALF), lambda g, x, p: (0, 0))
    return pl.pallas_call(
        short_kernel,
        out_shape=jax.ShapeDtypeStruct((2, 4, 4, 128, 128), F32),
        grid_spec=pltpu.PrefetchScalarGridSpec(
            num_scalar_prefetch=1,
            grid=(2, 4),
            in_specs=[left, left, right, right],
            out_specs=pl.BlockSpec((1, 4, 1, 128, 128), lambda g, x, p: (g, 0, x, 0, 0)),
        ),
        compiler_params=params(),
        cost_estimate=cost(2 * 1024 * 1024 * 512, 6 << 20),
        name="partial_y",
    )(pick, xo, xp, do, dp)


def heads_kernel(pick, xo_ref, xp_ref, doa_ref, dob_ref, dpa_ref, dpb_ref, o_ref):
    del pick
    own = jnp.concatenate([doa_ref[...], dob_ref[...]], 1)
    other = jnp.concatenate([dpa_ref[...], dpb_ref[...]], 1)
    total = dot(xo_ref[...], own, 1, 0) + dot(xp_ref[...], other, 1, 0)
    for g in range(2):
        for y in range(4):
            o_ref[g, 0, y] = total[y * 128 : (y + 1) * 128, g * 128 : (g + 1) * 128]


def partial_z(xo, xp, do, dp, pick):
    left = pl.BlockSpec((512, BLK), lambda x, p: (x, 0))
    first = pl.BlockSpec((BLK, DH), lambda x, p: (0, p[0]))
    second = pl.BlockSpec((BLK, DH), lambda x, p: (0, p[1]))
    return pl.pallas_call(
        heads_kernel,
        out_shape=jax.ShapeDtypeStruct((2, 4, 4, 128, 128), F32),
        grid_spec=pltpu.PrefetchScalarGridSpec(
            num_scalar_prefetch=1,
            grid=(4,),
            in_specs=[left, left, first, second, first, second],
            out_specs=pl.BlockSpec((2, 1, 4, 128, 128), lambda x, p: (0, x, 0, 0, 0)),
        ),
        compiler_params=params(),
        cost_estimate=cost(2 * 1024 * 1024 * 512, 6 << 20),
        name="partial_z",
    )(pick, xo, xp, do, do, dp, dp)


def tokens_back_kernel(core, dq_ref, dk_ref, dv_ref, back_ref, w_ref, o_ref, full_ref):
    for c in range(2):

        @pl.when(jnp.logical_and(pl.program_id(0) == 0, core[0] == c))
        def _():
            for kind, own in enumerate((dq_ref, dk_ref, dv_ref)):
                full_ref[:, pl.ds((2 * kind + c) * HALF, HALF)] = own[...]
                full_ref[:, pl.ds((2 * kind + 1 - c) * HALF, HALF)] = back_ref[kind].astype(BF16)

    o_ref[...] = dot(full_ref[...], w_ref[...], 1, 1).astype(BF16)


def tokens_back(dq, dk, dv, back, w, core):
    cols = 256
    own = pl.BlockSpec((BLK, HALF), lambda j, c: (0, 0))
    return pl.pallas_call(
        tokens_back_kernel,
        out_shape=jax.ShapeDtypeStruct((BLK, D), BF16),
        grid_spec=pltpu.PrefetchScalarGridSpec(
            num_scalar_prefetch=1,
            grid=(D // cols,),
            in_specs=[
                own,
                own,
                own,
                pl.BlockSpec((3, BLK, HALF), lambda j, c: (0, 0, 0)),
                pl.BlockSpec((cols, 3072), lambda j, c: (j, 0)),
            ],
            out_specs=pl.BlockSpec((BLK, cols), lambda j, c: (0, j)),
            scratch_shapes=[pltpu.VMEM((BLK, 3072), BF16)],
        ),
        compiler_params=params(),
        cost_estimate=cost(2 * BLK * D * 3072, 20 << 20),
        name="tokens_back",
    )(core, dq, dk, dv, back, w)


def at(value, i):
    return lax.dynamic_index_in_dim(value, i, 0, keepdims=False)


def body(tokens, w_qkv, cotangent):
    s = lax.axis_index("seq")
    z = lax.axis_index("batch")
    c = s % 2
    chip = s // 2
    x = chip // 4
    y = chip % 4
    core = c.reshape(1)
    own_x = tokens[0]
    other_wide = permute(own_x.astype(F32), core_pairs())
    position = s * BLK + jnp.arange(BLK, dtype=jnp.int32)
    pos_scale = DH ** (-0.5) / jnp.sqrt(position.astype(F32) + 1.0)
    scaled = (cotangent[0].astype(F32) * pos_scale[:, None]).astype(BF16)
    own_g = lax.dynamic_slice_in_dim(scaled, c * HALF, HALF, 1)
    sent_g = lax.dynamic_slice_in_dim(scaled, (1 - c) * HALF, HALF, 1).astype(F32)
    other_g_wide = permute(sent_g, core_pairs())
    (own_p,) = project(own_x, w_qkv, core)
    own_st, own_low = states(own_p, own_g)
    other_p, other_x = project(other_wide, w_qkv, core)
    other_st, other_low = states(other_p, other_g_wide)
    chip_st = own_st + other_st
    got = [at(chip_st, y)]
    for d in range(1, 4):
        got.append(permute(at(chip_st, (y + d) % 4), shift_pairs("y", d)))
    row_kv = got[0][0] + got[1][0] + got[2][0] + got[3][0]
    row_gr = got[0][1] + got[1][1] + got[2][1] + got[3][1]
    enter_kv = jnp.zeros_like(row_kv)
    enter_gr = jnp.zeros_like(row_gr)
    for d in range(1, 4):
        came = permute(jnp.where(x + d < 4, row_kv, row_gr), shift_pairs("x", d))
        earlier = x - d >= 0
        enter_kv = enter_kv + jnp.where(earlier, came, 0.0)
        enter_gr = enter_gr + jnp.where(earlier, 0.0, came)
    back = []
    for e in range(4):
        there = (y + e) % 4
        kv, gr = enter_kv, enter_gr
        for d in range(4):
            here = (y - d + 4) % 4
            kv = kv + jnp.where(here < there, got[d][0], 0.0)
            gr = gr + jnp.where(here > there, got[d][1], 0.0)
        back.append(jnp.stack([kv, gr]))
    mine = [back[0]]
    for e in range(1, 4):
        mine.append(permute(back[e], shift_pairs("y", e)))
    state_in = jnp.stack(mine)
    order = (y - jnp.arange(4) + 4) % 4
    own_rolled = jnp.stack([at(own_st, order[j]) for j in range(4)])
    other_rolled = jnp.stack([at(other_st, order[j]) for j in range(4)])
    cf = c.astype(F32)
    pick_kv = jnp.stack([cf, 1.0 - cf]).reshape(1, 2, 1, 1)
    own_state = state_in + pick_kv * other_rolled
    other_state = state_in + (1.0 - pick_kv) * own_rolled
    own_parts = intra(own_p, own_low)
    other_parts = intra(other_p, other_low)
    xo = turned(own_x)
    xp = turned(other_x)
    own_att, own_dq, own_dk, own_dv = inter(
        own_p, own_low, own_parts, own_state, jnp.stack([y, s * BLK]), BF16
    )
    other_att, other_dq, other_dk, other_dv = inter(
        other_p, other_low, other_parts, other_state, jnp.stack([y, (s ^ 1) * BLK]), F32
    )
    place = dict(x=x, y=y, z=z)

    def picks(axis):
        v = place[axis]
        w1, w2 = partner(v, c), partner(v, 1 - c)
        return jnp.stack([w1, partner(w1, 1 - c)]), jnp.stack([v, w2])

    thirds = [
        ("xyz", partial_x, own_dq, other_dq),
        ("yzx", partial_y, own_dk, other_dk),
        ("zxy", partial_z, own_dv, other_dv),
    ]
    held = []
    for order_, make, do, dp in thirds:
        send_pick, keep_pick = picks(order_[0])
        sent = make(xo, xp, do, dp, send_pick)
        came = permute(sent, halving_pairs(order_[0], 0))
        kept = make(xo, xp, do, dp, keep_pick)
        held.append((kept, came))
    held = [
        kept[0] + came[0] + permute(kept[1] + came[1], halving_pairs(order_[0], 1))
        for (kept, came), (order_, *_) in zip(held, thirds)
    ]
    for step in (1, 2):
        after = []
        for value, (order_, *_) in zip(held, thirds):
            axis = order_[step]
            send_pick, keep_pick = picks(axis)
            sent = jnp.stack([at(value, send_pick[0]), at(value, send_pick[1])])
            came = permute(sent, halving_pairs(axis, 0))
            first = at(value, keep_pick[0]) + came[0]
            second = at(value, keep_pick[1]) + came[1]
            after.append(first + permute(second, halving_pairs(axis, 1)))
        held = after
    grad_scale = 1.0 / jnp.sqrt(F32(65536.0))
    mine_w = jnp.stack(held) * grad_scale
    mine_w = mine_w.reshape(3, 2, 64, 128)
    to_other = lax.dynamic_index_in_dim(mine_w, 1 - c, 1, keepdims=False)
    own_w = lax.dynamic_index_in_dim(mine_w, c, 1, keepdims=False)
    from_other = permute(to_other, core_pairs())
    pair = jnp.stack([jnp.where(c == 0, own_w, from_other), jnp.where(c == 0, from_other, own_w)], 1)
    all_z = [pair]
    for d in range(1, 4):
        all_z.append(permute(pair, shift_pairs("z", d)))
    stacked = jnp.stack(all_z)
    ordered = jnp.stack([at(stacked, (z - h + 4) % 4) for h in range(4)])
    weight_grad = ordered.transpose(3, 1, 2, 0, 4).reshape(64, 3072)
    att_back = permute(other_att, core_pairs())
    own_wide = own_att.astype(F32)
    att_back = att_back * pos_scale[:, None]
    attended = jnp.concatenate(
        [jnp.where(c == 0, own_wide, att_back), jnp.where(c == 0, att_back, own_wide)], 1
    ).astype(BF16)
    back_d = permute(
        jnp.stack([other_dq.astype(F32), other_dk.astype(F32), other_dv.astype(F32)]), core_pairs()
    )
    token_grad = tokens_back(own_dq, own_dk, own_dv, back_d, w_qkv, core)
    return attended[None], token_grad[None], weight_grad


def solution(mesh):
    return jax.shard_map(
        body,
        mesh=mesh,
        in_specs=(P("batch", "seq", None), P(), P("batch", "seq", None)),
        out_specs=(P("batch", "seq", None), P("batch", "seq", None), P("seq", None)),
        check_vma=False,
    )
```

```python
import jax
import jax.numpy as jnp
import numpy as np
from jax import lax
from jax.experimental import pallas as pl
from jax.experimental.pallas import tpu as pltpu
from jax.sharding import PartitionSpec as P

DH = 128
BLK = 512
D = 2048
HALF = 512
NEAR = 4
F32 = jnp.float32
BF16 = jnp.bfloat16
AXES = ("seq", "batch")
VMEM = 16 * 1024 * 1024
CORE, X, Y, Z, BASE, OTHER_BASE = range(6)
PICKS = dict(x=6, y=10, z=14)


def flat(x, y, c, z):
    return ((x * 4 + y) * 2 + c) * 4 + z


def every():
    for x in range(4):
        for y in range(4):
            for c in range(2):
                for z in range(4):
                    yield x, y, c, z


def partner(v, kind):
    return v ^ 1 if kind == 0 else 3 - v


def table():
    rows = np.zeros((128, 18), np.int32)
    for x, y, c, z in every():
        s = (x * 4 + y) * 2 + c
        row = [c, x, y, z, s * BLK, (s ^ 1) * BLK]
        for v in (x, y, z):
            w = partner(v, c)
            row += [w, partner(w, 1 - c), v, partner(v, 1 - c)]
        rows[flat(x, y, c, z)] = row
    return rows


def shift_pairs(axis, d):
    pairs = []
    for x, y, c, z in every():
        to = dict(x=x, y=y, z=z)
        to[axis] = (to[axis] + d) % 4
        pairs.append((flat(x, y, c, z), flat(to["x"], to["y"], c, to["z"])))
    return pairs


def core_pairs():
    return [(flat(x, y, c, z), flat(x, y, 1 - c, z)) for x, y, c, z in every()]


def halving_pairs(axis, step):
    pairs = []
    for x, y, c, z in every():
        to = dict(x=x, y=y, z=z)
        to[axis] = partner(to[axis], (c + step) % 2)
        pairs.append((flat(x, y, c, z), flat(to["x"], to["y"], c, to["z"])))
    return pairs


def permute(value, pairs):
    return lax.ppermute(value, AXES, pairs)


def dot(a, b, contract_a, contract_b):
    return lax.dot_general(
        a, b, (((contract_a,), (contract_b,)), ((), ())), preferred_element_type=F32
    )


WHOLE = pl.BlockSpec(memory_space=pltpu.VMEM)
SCALARS = pl.BlockSpec(memory_space=pltpu.SMEM)
PLACED = pl.BlockSpec(memory_space=pltpu.MemorySpace.HBM)


def call(name, kernel, info, args, outs, scratch=(), stay=()):
    specs = [PLACED if i in stay else WHOLE for i in range(len(args))]
    args = [
        pltpu.with_memory_space_constraint(a, pltpu.HBM) if i in stay else a for i, a in enumerate(args)
    ]
    if info is not None:
        specs = [SCALARS] + specs
        args = [info] + args
    return pl.pallas_call(
        kernel,
        out_shape=[jax.ShapeDtypeStruct(shape, kind) for shape, kind in outs],
        in_specs=specs,
        out_specs=[WHOLE] * len(outs),
        scratch_shapes=list(scratch),
        compiler_params=pltpu.CompilerParams(vmem_limit_bytes=VMEM),
        cost_estimate=pl.CostEstimate(flops=1, bytes_accessed=1, transcendentals=0),
        name=name,
    )(*args)


def scale_of(base):
    position = base + lax.broadcasted_iota(jnp.int32, (BLK, DH), 0)
    return DH ** (-0.5) / jnp.sqrt(position.astype(F32) + 1.0)


def widen_kernel(half):
    def kernel(x_ref, o_ref):
        o_ref[...] = x_ref[half * 256 : half * 256 + 256, :].astype(F32)

    return kernel


def grad_kernel(info, cot_ref, own_ref, sent_ref):
    scale = scale_of(info[BASE])
    for c in range(2):

        @pl.when(info[CORE] == c)
        def _():
            for h in range(NEAR):
                to = slice(h * DH, h * DH + DH)
                for first, ref in ((c * HALF, own_ref), ((1 - c) * HALF, sent_ref)):
                    at = slice(first + h * DH, first + h * DH + DH)
                    low = (cot_ref[:, at].astype(F32) * scale).astype(BF16)
                    ref[:, to] = low.astype(ref.dtype)


def project_kernel(info, x_ref, w_ref, p_ref, wo_ref, sems):
    def copy(j):
        at = pl.multiple_of((2 * j + info[CORE]) * HALF, HALF)
        return pltpu.make_async_copy(
            w_ref.at[:, pl.ds(at, HALF)], wo_ref.at[:, pl.ds(j * HALF, HALF)], sems.at[j]
        )

    for j in range(3):
        copy(j).start()
    for j in range(3):
        copy(j).wait()
        at = slice(j * HALF, (j + 1) * HALF)
        p_ref[:, at] = dot(x_ref[...], wo_ref[:, at], 1, 0).astype(BF16)


def project_first_kernel(x_ref, w_ref, p_ref, low_ref):
    low_ref[...] = x_ref[...].astype(BF16)
    for j in range(3):
        at = slice(j * HALF, (j + 1) * HALF)
        p_ref[:, at] = dot(low_ref[...], w_ref[:, at], 1, 0).astype(BF16)


def project_second_kernel(x_ref, w_ref, p0_ref, low0_ref, p_ref, low_ref):
    low_ref[0:256, :] = low0_ref[...]
    low_ref[256:512, :] = x_ref[...].astype(BF16)
    p_ref[0:256, :] = p0_ref[...]
    for j in range(3):
        at = slice(j * HALF, (j + 1) * HALF)
        p_ref[256:512, at] = dot(low_ref[256:512, :], w_ref[:, at], 1, 0).astype(BF16)


def head(kind, h):
    return slice(kind * HALF + h * DH, kind * HALF + h * DH + DH)


def states_kernel(p_ref, g_ref, st_ref):
    for h in range(NEAR):
        st_ref[h, 0] = dot(p_ref[:, head(1, h)], p_ref[:, head(2, h)], 0, 0)
        st_ref[h, 1] = dot(p_ref[:, head(0, h)], g_ref[:, head(0, h)], 0, 0)


def chip_states_kernel(info, p_ref, gw_ref, own_ref, low_ref, st_ref, o0, o1, o2, o3, sum_ref):
    low_ref[...] = gw_ref[...].astype(BF16)
    for h in range(NEAR):
        kv = dot(p_ref[:, head(1, h)], p_ref[:, head(2, h)], 0, 0)
        gr = dot(p_ref[:, head(0, h)], low_ref[:, head(0, h)], 0, 0)
        st_ref[h, 0] = kv
        st_ref[h, 1] = gr
        sum_ref[h, 0] = kv + own_ref[h, 0]
        sum_ref[h, 1] = gr + own_ref[h, 1]
    for d, ref in enumerate((o0, o1, o2, o3)):
        ref[...] = sum_ref[(info[Y] + d) % 4]


def row_kernel(info, g0, g1, g2, g3, o1, o2, o3):
    kv = g0[0] + g1[0] + g2[0] + g3[0]
    gr = g0[1] + g1[1] + g2[1] + g3[1]
    for d, ref in ((1, o1), (2, o2), (3, o3)):
        ref[...] = jnp.where(info[X] + d < 4, kv, gr)


def back_kernel(info, g0, g1, g2, g3, c1, c2, c3, o0, o1, o2, o3):
    enter_kv = jnp.zeros((DH, DH), F32)
    enter_gr = jnp.zeros((DH, DH), F32)
    for d, ref in ((1, c1), (2, c2), (3, c3)):
        earlier = info[X] >= d
        enter_kv = enter_kv + jnp.where(earlier, ref[...], 0.0)
        enter_gr = enter_gr + jnp.where(earlier, 0.0, ref[...])
    for e, out in enumerate((o0, o1, o2, o3)):
        there = (info[Y] + e) % 4
        kv, gr = enter_kv, enter_gr
        for d, ref in enumerate((g0, g1, g2, g3)):
            here = (info[Y] + 4 - d) % 4
            kv = kv + jnp.where(here < there, ref[0], 0.0)
            gr = gr + jnp.where(here > there, ref[1], 0.0)
        out[0] = kv
        out[1] = gr


def intra_kernel(pair):
    def kernel(p_ref, g_ref, att_ref, dq_ref, dk_ref, dv_ref):
        rows = lax.broadcasted_iota(jnp.int32, (BLK, BLK), 0)
        cols = lax.broadcasted_iota(jnp.int32, (BLK, BLK), 1)
        causal = rows >= cols
        for i in range(2):
            h = 2 * pair + i
            to = slice(i * DH, i * DH + DH)
            q, k, v = (p_ref[:, head(kind, h)] for kind in range(3))
            g = g_ref[:, head(0, h)]
            scores = jnp.where(causal, dot(q, k, 1, 1), 0.0).astype(BF16)
            att_ref[:, to] = dot(scores, v, 1, 0)
            dv_ref[:, to] = dot(scores, g, 0, 0)
            grad_scores = jnp.where(causal, dot(g, v, 1, 1), 0.0).astype(BF16)
            dq_ref[:, to] = dot(grad_scores, k, 1, 0)
            dk_ref[:, to] = dot(grad_scores, q, 0, 0)

    return kernel


def turn_kernel(own_ref, other_ref, o_ref):
    for j in range(4):
        at = slice(j * 512, j * 512 + 512)
        o_ref[at, 0:512] = own_ref[:, at].T
        o_ref[at, 512:1024] = other_ref[:, at].T


def settle_kernel(info, m0, m1, m2, m3, own_ref, other_ref, o_ref):
    c = info[CORE].astype(F32)
    o_ref[...] = jnp.zeros(o_ref.shape, BF16)
    for j, ref in enumerate((m0, m1, m2, m3)):
        for h in range(NEAR):

            @pl.when((info[Y] + 4 - j) % 4 == h)
            def _():
                at = slice((h % 2) * DH, (h % 2) * DH + DH)
                o_ref[0, h // 2, 0, at, at] = (ref[0] + c * other_ref[h, 0]).astype(BF16)
                o_ref[0, h // 2, 1, at, at] = (ref[1] + (1.0 - c) * other_ref[h, 1]).astype(BF16)
                o_ref[1, h // 2, 0, at, at] = (ref[0] + (1.0 - c) * own_ref[h, 0]).astype(BF16)
                o_ref[1, h // 2, 1, at, at] = (ref[1] + c * own_ref[h, 1]).astype(BF16)


def pair_of(kind, pair):
    return slice(kind * HALF + pair * 256, kind * HALF + pair * 256 + 256)


def rows_of(block):
    return slice(block * BLK, block * BLK + BLK)


def query_kernel(info, st_ref, go_ref, gp_ref, d00, d01, d10, d11, xt_ref, dq_ref, o_ref):
    parts = ((d00, d01), (d10, d11))
    for block, g_ref in enumerate((go_ref, gp_ref)):
        for pair in range(2):
            at = pair_of(0, pair)
            far = dot(g_ref[:, at], st_ref[block, pair, 0], 1, 1)
            dq_ref[rows_of(block), at] = (parts[block][pair][...] + far).astype(BF16)
    partial_x_kernel(0)(info, xt_ref, dq_ref, o_ref)


def key_value_kernel(
    info, st_ref, po_ref, pp_ref, k00, k01, k10, k11, v00, v01, v10, v11, xt_ref, dq_ref, dk_ref, dv_ref, o_ref, wide_ref
):
    keys = ((k00, k01), (k10, k11))
    values = ((v00, v01), (v10, v11))
    for block, p_ref in enumerate((po_ref, pp_ref)):
        for pair in range(2):
            at = pair_of(0, pair)
            gr = st_ref[block, pair, 1]
            far = dot(p_ref[:, pair_of(2, pair)], gr, 1, 1)
            dk_ref[rows_of(block), at] = (keys[block][pair][...] + far).astype(BF16)
            far = dot(p_ref[:, pair_of(1, pair)], gr, 1, 0)
            dv_ref[rows_of(block), at] = (values[block][pair][...] + far).astype(BF16)
    partial_y_kernel(0)(info, xt_ref, dk_ref, o_ref)
    for kind, ref in enumerate((dq_ref, dk_ref, dv_ref)):
        wide_ref[kind] = ref[512:1024, :].astype(F32)


def attend_kernel(info, st_ref, po_ref, pp_ref, a00, a01, a10, a11, own_ref, other_ref):
    parts = ((a00, a01), (a10, a11))
    scale = scale_of(info[BASE])
    for block, p_ref in enumerate((po_ref, pp_ref)):
        for pair in range(2):
            at = pair_of(0, pair)
            total = parts[block][pair][...] + dot(p_ref[:, at], st_ref[block, pair, 0], 1, 0)
            if block == 0:
                for i in range(2):
                    to = slice(pair * 256 + i * DH, pair * 256 + i * DH + DH)
                    own_ref[:, to] = (total[:, i * DH : i * DH + DH] * scale).astype(BF16)
            else:
                other_ref[:, at] = total


def attended_kernel(info, own_ref, back_ref, o_ref):
    scale = scale_of(info[BASE])
    for c in range(2):

        @pl.when(info[CORE] == c)
        def _():
            o_ref[:, c * HALF : c * HALF + HALF] = own_ref[...]
            for h in range(NEAR):
                to = slice((1 - c) * HALF + h * DH, (1 - c) * HALF + h * DH + DH)
                o_ref[:, to] = (back_ref[:, head(0, h)] * scale).astype(BF16)


def partial_x_kernel(keep):
    def kernel(info, xt_ref, d_ref, o_ref):
        for g in range(2):
            at = pl.multiple_of(info[PICKS["x"] + 2 * keep + g] * 512, 512)
            total = dot(xt_ref[pl.ds(at, 512), :], d_ref[...], 1, 0)
            for y in range(4):
                for z in range(4):
                    o_ref[g, y, z] = total[y * 128 : y * 128 + 128, z * 128 : z * 128 + 128]

    return kernel


def partial_y_kernel(keep):
    def kernel(info, xt_ref, d_ref, o_ref):
        for g in range(2):
            y = info[PICKS["y"] + 2 * keep + g]
            left = [xt_ref[pl.ds(pl.multiple_of(x * 512 + y * 128, 128), 128), :] for x in range(4)]
            total = dot(jnp.concatenate(left, 0), d_ref[...], 1, 0)
            for x in range(4):
                for z in range(4):
                    o_ref[g, z, x] = total[x * 128 : x * 128 + 128, z * 128 : z * 128 + 128]

    return kernel


def partial_z_kernel(keep):
    def kernel(info, xt_ref, d_ref, o_ref):
        right = []
        for g in range(2):
            at = pl.multiple_of(info[PICKS["z"] + 2 * keep + g] * 128, 128)
            right.append(d_ref[:, pl.ds(at, 128)])
        right = jnp.concatenate(right, 1)
        for x in range(4):
            total = dot(xt_ref[x * 512 : x * 512 + 512, :], right, 1, 0)
            for g in range(2):
                for y in range(4):
                    o_ref[g, x, y] = total[y * 128 : y * 128 + 128, g * 128 : g * 128 + 128]

    return kernel


def tokens_out_kernel(info, dq_ref, dk_ref, dv_ref, back_ref, wo_ref, w_ref, o_ref, d_ref, wp_ref, sems):
    def copy(j, kind):
        at = pl.multiple_of((2 * kind + 1 - info[CORE]) * HALF, HALF)
        rows = pl.ds(j * 512, 512)
        return pltpu.make_async_copy(
            w_ref.at[rows, pl.ds(at, HALF)],
            wp_ref.at[rows, pl.ds(kind * HALF, HALF)],
            sems.at[3 * j + kind],
        )

    for j in range(4):
        for kind in range(3):
            copy(j, kind).start()
    for kind, ref in enumerate((dq_ref, dk_ref, dv_ref)):
        at = slice(kind * HALF, kind * HALF + HALF)
        d_ref[0, :, at] = ref[0:512, :]
        d_ref[1, :, at] = back_ref[kind].astype(BF16)
    for j in range(4):
        at = slice(j * 512, j * 512 + 512)
        own = dot(d_ref[0], wo_ref[at, :], 1, 1)
        for kind in range(3):
            copy(j, kind).wait()
        o_ref[:, at] = (own + dot(d_ref[1], wp_ref[at, :], 1, 1)).astype(BF16)


def second_kernel(kept_ref, came_ref, o_ref):
    o_ref[...] = kept_ref[1] + came_ref[1]


def regroup_kernel(axis):
    def kernel(info, kept_ref, came_ref, more_ref, sent_ref, keep_ref):
        for g in range(4):
            i = info[PICKS[axis] + g]
            out = sent_ref if g < 2 else keep_ref
            out[g % 2] = kept_ref[0, i] + came_ref[0, i] + more_ref[i]

    return kernel


def rows_out_kernel(info, *refs):
    to_ref, own_ref = refs[9], refs[10]
    for third in range(3):
        kept_ref, came_ref, more_ref = refs[3 * third : 3 * third + 3]
        total = (kept_ref[0] + came_ref[0] + more_ref[...]) * (1.0 / 256.0)
        for c in range(2):

            @pl.when(info[CORE] == c)
            def _():
                own_ref[third] = total[c * 64 : c * 64 + 64]
                to_ref[third] = total[(1 - c) * 64 : (1 - c) * 64 + 64]


def both_cores_kernel(info, own_ref, came_ref, o_ref):
    for c in range(2):

        @pl.when(info[CORE] == c)
        def _():
            for third in range(3):
                o_ref[third, c] = own_ref[third]
                o_ref[third, 1 - c] = came_ref[third]


def weight_kernel(info, a0, a1, a2, a3, o_ref):
    for d, ref in enumerate((a0, a1, a2, a3)):
        z = (info[Z] + 4 - d) % 4
        for third in range(3):
            for c in range(2):
                first = third * 1024 + c * HALF
                o_ref[:, pl.ds(pl.multiple_of(first + z * DH, DH), DH)] = ref[third, c]


def after(values, done):
    return lax.optimization_barrier((values, done))[0]


def body(tokens, w_qkv, cotangent):
    device = lax.axis_index("seq") * 4 + lax.axis_index("batch")
    info = lax.dynamic_index_in_dim(jnp.asarray(table()), device, 0, keepdims=False)
    own_x = tokens[0]
    square = (2, DH, DH)
    wide = []
    for half in range(2):
        (mine,) = call("widen", widen_kernel(half), None, [own_x], [((256, D), F32)])
        wide.append(permute(mine, core_pairs()))
    own_g, sent_g = call(
        "grad", grad_kernel, info, [cotangent[0]], [((BLK, HALF), BF16), ((BLK, HALF), F32)]
    )
    other_gw = permute(sent_g, core_pairs())
    own_p, w_own = call(
        "project",
        project_kernel,
        info,
        [own_x, w_qkv],
        [((BLK, 3 * HALF), BF16), ((D, 3 * HALF), BF16)],
        scratch=[pltpu.SemaphoreType.DMA((3,))],
        stay=(1,),
    )
    (own_st,) = call("states", states_kernel, None, [own_p, own_g], [((NEAR,) + square, F32)])
    quarter = ((BLK, 256), F32)

    def intra(pair, p, g):
        return call("intra", intra_kernel(pair), None, [p, g], [quarter] * 4)

    own_parts = [intra(0, *after((own_p, own_g), own_st))]
    wide[0] = after(wide[0], own_parts[0])
    p0, low0 = call(
        "project_first",
        project_first_kernel,
        None,
        [wide[0], w_own],
        [((256, 3 * HALF), BF16), ((256, D), BF16)],
    )
    other_p, other_x = call(
        "project_second",
        project_second_kernel,
        None,
        [wide[1], w_own, p0, low0],
        [((BLK, 3 * HALF), BF16), ((BLK, D), BF16)],
    )
    other_g, other_st, *pay = call(
        "chip_states",
        chip_states_kernel,
        info,
        [other_p, other_gw, own_st],
        [((BLK, HALF), BF16), ((NEAR,) + square, F32)] + [(square, F32)] * 4,
        scratch=[pltpu.VMEM((NEAR,) + square, F32)],
    )
    got = [pay[0]] + [permute(pay[d], shift_pairs("y", d)) for d in range(1, 4)]
    other_parts = [intra(0, *after((other_p, other_g), pay))]
    got = after(got, other_parts)
    rows = call("row", row_kernel, info, got, [((DH, DH), F32)] * 3)
    came = [permute(rows[d - 1], shift_pairs("x", d)) for d in range(1, 4)]
    own_parts.append(intra(1, *after((own_p, own_g), rows)))
    came = after(came, own_parts[1])
    back = call("back", back_kernel, info, got + came, [(square, F32)] * 4)
    mine = [back[0]] + [permute(back[e], shift_pairs("y", e)) for e in range(1, 4)]
    other_parts.append(intra(1, *after((other_p, other_g), back)))
    (xt,) = call("turn", turn_kernel, None, after([own_x, other_x], back), [((D, 1024), BF16)])
    mine = after(mine, (other_parts[1], xt))
    (state,) = call(
        "settle", settle_kernel, info, mine + [own_st, other_st], [((2, 2, 2, 256, 256), BF16)]
    )
    parts = [[own_parts[0][i], own_parts[1][i], other_parts[0][i], other_parts[1][i]] for i in range(4)]
    tall = ((1024, HALF), BF16)
    group = ((2, 4, 4, 128, 128), F32)
    dq, sent_x = call(
        "query", query_kernel, info, [state, own_g, other_g] + parts[1] + [xt], [tall, group]
    )
    came_x = permute(sent_x, halving_pairs("x", 0))
    dk, dv, sent_y, wide_d = call(
        "key_value",
        key_value_kernel,
        info,
        [state, own_p, other_p] + parts[2] + parts[3] + [xt, dq],
        [tall, tall, group, ((3, BLK, HALF), F32)],
    )
    came_y = permute(sent_y, halving_pairs("y", 0))
    (sent_z,) = call("partial_z", partial_z_kernel(0), info, [xt, dv], [group])
    came_z = permute(sent_z, halving_pairs("z", 0))
    (kept_x,) = call("partial_x", partial_x_kernel(1), info, after([xt, dq], sent_z), [group])
    (kept_y,) = call("partial_y", partial_y_kernel(1), info, after([xt, dk], kept_x), [group])
    (kept_z,) = call("partial_z", partial_z_kernel(1), info, after([xt, dv], kept_y), [group])
    back_d = permute(wide_d, core_pairs())
    own_att, other_att = call(
        "attend",
        attend_kernel,
        info,
        [after(state, kept_z), own_p, other_p] + parts[0],
        [((BLK, HALF), BF16), ((BLK, HALF), F32)],
    )
    att_back = permute(other_att, core_pairs())
    came_x, came_y, came_z = after((came_x, came_y, came_z), own_att)
    thirds = [
        ["xyz", kept_x, came_x],
        ["yzx", kept_y, came_y],
        ["zxy", kept_z, came_z],
    ]
    for step in range(3):
        for third in thirds:
            axes, kept, came = third[:3]
            (pay,) = call("second", second_kernel, None, [kept, came], [(kept.shape[1:], F32)])
            third.append(permute(pay, halving_pairs(axes[step], 1)))
        if step == 0:
            args = after([dq, dk, dv, back_d, att_back], pay)
            (token_grad,) = call(
                "tokens_out",
                tokens_out_kernel,
                info,
                args[:4] + [w_own, w_qkv],
                [((BLK, D), BF16)],
                scratch=[
                    pltpu.VMEM((2, BLK, 3 * HALF), BF16),
                    pltpu.VMEM((D, 3 * HALF), BF16),
                    pltpu.SemaphoreType.DMA((12,)),
                ],
                stay=(5,),
            )
            (attended,) = call(
                "attended",
                attended_kernel,
                info,
                [own_att, after(args[4], token_grad)],
                [((BLK, 2 * HALF), BF16)],
            )
            for third in thirds:
                third[3] = after(third[3], attended)
        if step < 2:
            for third in thirds:
                axes, kept, came, more = third
                outs = [((2,) + kept.shape[2:], F32)] * 2
                sent, keep = call(
                    "regroup", regroup_kernel(axes[step + 1]), info, [kept, came, more], outs
                )
                third[1:] = [keep, permute(sent, halving_pairs(axes[step + 1], 0))]
    to_other, own_w = call(
        "rows_out",
        rows_out_kernel,
        info,
        [part for third in thirds for part in third[1:]],
        [((3, 64, DH), F32)] * 2,
    )
    from_other = permute(to_other, core_pairs())
    (pair,) = call("both_cores", both_cores_kernel, info, [own_w, from_other], [((3, 2, 64, DH), F32)])
    along = [pair] + [permute(pair, shift_pairs("z", d)) for d in range(1, 4)]
    (weight_grad,) = call("weight", weight_kernel, info, along, [((64, 3072), F32)])
    return attended[None], token_grad[None], weight_grad


def solution(mesh):
    return jax.shard_map(
        body,
        mesh=mesh,
        in_specs=(P("batch", "seq", None), P(), P("batch", "seq", None)),
        out_specs=(P("batch", "seq", None), P("batch", "seq", None), P("seq", None)),
        check_vma=False,
    )
```

```python
import jax
import jax.numpy as jnp
import numpy as np
from jax import lax
from jax.experimental import pallas as pl
from jax.experimental.pallas import tpu as pltpu
from jax.sharding import PartitionSpec as P

DH = 128
BLK = 512
D = 2048
HALF = 512
NEAR = 4
F32 = jnp.float32
BF16 = jnp.bfloat16
SPREAD = True
AXES = ("seq", "batch")
VMEM = 16 * 1024 * 1024
CORE, X, Y, Z, BASE, OTHER_BASE = range(6)
PICKS = dict(x=6, y=10, z=14)
SLOTS = dict(x=18, y=22, z=26)


def flat(x, y, c, z):
    return ((x * 4 + y) * 2 + c) * 4 + z


def every():
    for x in range(4):
        for y in range(4):
            for c in range(2):
                for z in range(4):
                    yield x, y, c, z


def partner(v, kind):
    return v ^ 1 if kind == 0 else 3 - v


def table():
    rows = np.zeros((128, 30), np.int32)
    for x, y, c, z in every():
        s = (x * 4 + y) * 2 + c
        row = [c, x, y, z, s * BLK, (s ^ 1) * BLK]
        for v in (x, y, z):
            w = partner(v, c)
            row += [w, partner(w, 1 - c), v, partner(v, 1 - c)]
        for first in (6, 10, 14):
            row += [row[first : first + 4].index(i) for i in range(4)]
        rows[flat(x, y, c, z)] = row
    return rows


def shift_pairs(axis, d, swap=False):
    pairs = []
    for x, y, c, z in every():
        to = dict(x=x, y=y, z=z)
        to[axis] = (to[axis] + d) % 4
        pairs.append((flat(x, y, c, z), flat(to["x"], to["y"], c ^ int(swap), to["z"])))
    return pairs


def core_pairs():
    return [(flat(x, y, c, z), flat(x, y, 1 - c, z)) for x, y, c, z in every()]


def halving_pairs(axis, step):
    pairs = []
    for x, y, c, z in every():
        to = dict(x=x, y=y, z=z)
        to[axis] = partner(to[axis], (c + step) % 2)
        pairs.append((flat(x, y, c, z), flat(to["x"], to["y"], c, to["z"])))
    return pairs


def permute(value, pairs):
    return lax.ppermute(value, AXES, pairs)


def dot(a, b, contract_a, contract_b):
    return lax.dot_general(
        a, b, (((contract_a,), (contract_b,)), ((), ())), preferred_element_type=F32
    )


WHOLE = pl.BlockSpec(memory_space=pltpu.VMEM)
SCALARS = pl.BlockSpec(memory_space=pltpu.SMEM)
PLACED = pl.BlockSpec(memory_space=pltpu.MemorySpace.HBM)


def call(name, kernel, info, args, outs, scratch=(), stay=()):
    specs = [PLACED if i in stay else WHOLE for i in range(len(args))]
    args = [
        pltpu.with_memory_space_constraint(a, pltpu.HBM) if i in stay else a for i, a in enumerate(args)
    ]
    if info is not None:
        specs = [SCALARS] + specs
        args = [info] + args
    return pl.pallas_call(
        kernel,
        out_shape=[jax.ShapeDtypeStruct(shape, kind) for shape, kind in outs],
        in_specs=specs,
        out_specs=[WHOLE] * len(outs),
        scratch_shapes=list(scratch),
        compiler_params=pltpu.CompilerParams(vmem_limit_bytes=VMEM),
        cost_estimate=pl.CostEstimate(flops=1, bytes_accessed=1, transcendentals=0),
        name=name,
    )(*args)


def scale_of(base):
    position = base + lax.broadcasted_iota(jnp.int32, (BLK, DH), 0)
    return DH ** (-0.5) / jnp.sqrt(position.astype(F32) + 1.0)


def widen_kernel(x_ref, o_ref):
    o_ref[...] = x_ref[...].astype(F32)


def grad_kernel(info, cot_ref, w_ref, own_ref, sent_ref, wo_ref, sems):
    def copy(j):
        at = pl.multiple_of((2 * j + info[CORE]) * HALF, HALF)
        return pltpu.make_async_copy(
            w_ref.at[:, pl.ds(at, HALF)], wo_ref.at[:, pl.ds(j * HALF, HALF)], sems.at[j]
        )

    for j in range(3):
        copy(j).start()
    scale = scale_of(info[BASE])
    for c in range(2):

        @pl.when(info[CORE] == c)
        def _():
            for h in range(NEAR):
                to = slice(h * DH, h * DH + DH)
                for first, ref in ((c * HALF, own_ref), ((1 - c) * HALF, sent_ref)):
                    at = slice(first + h * DH, first + h * DH + DH)
                    low = (cot_ref[:, at].astype(F32) * scale).astype(BF16)
                    ref[:, to] = low.astype(ref.dtype)

    for j in range(3):
        copy(j).wait()


def project_kernel(x_ref, w_ref, p_ref):
    for j in range(3):
        at = slice(j * HALF, (j + 1) * HALF)
        p_ref[:, at] = dot(x_ref[...], w_ref[:, at], 1, 0).astype(BF16)


def project_wide_kernel(x_ref, w_ref, p_ref, low_ref):
    low_ref[...] = x_ref[...].astype(BF16)
    for j in range(3):
        at = slice(j * HALF, (j + 1) * HALF)
        p_ref[:, at] = dot(low_ref[...], w_ref[:, at], 1, 0).astype(BF16)


def head(kind, h):
    return slice(kind * HALF + h * DH, kind * HALF + h * DH + DH)


def states_kernel(p_ref, g_ref, st_ref):
    for h in range(NEAR):
        st_ref[h, 0] = dot(p_ref[:, head(1, h)], p_ref[:, head(2, h)], 0, 0)
        st_ref[h, 1] = dot(p_ref[:, head(0, h)], g_ref[:, head(0, h)], 0, 0)


def chip_states_kernel(info, p_ref, gw_ref, own_ref, low_ref, st_ref, o0, o1, o2, o3, sum_ref):
    low_ref[...] = gw_ref[...].astype(BF16)
    for h in range(NEAR):
        kv = dot(p_ref[:, head(1, h)], p_ref[:, head(2, h)], 0, 0)
        gr = dot(p_ref[:, head(0, h)], low_ref[:, head(0, h)], 0, 0)
        st_ref[h, 0] = kv
        st_ref[h, 1] = gr
        sum_ref[h, 0] = kv + own_ref[h, 0]
        sum_ref[h, 1] = gr + own_ref[h, 1]
    for d, ref in enumerate((o0, o1, o2, o3)):
        ref[...] = sum_ref[(info[Y] + d) % 4]


def row_kernel(info, g0, g1, g2, g3, o1, o2, o3):
    kv = g0[0] + g1[0] + g2[0] + g3[0]
    gr = g0[1] + g1[1] + g2[1] + g3[1]
    for d, ref in ((1, o1), (2, o2), (3, o3)):
        ref[...] = jnp.where(info[X] + d < 4, kv, gr)


def back_kernel(info, g0, g1, g2, g3, c1, c2, c3, o0, o1, o2, o3):
    enter_kv = jnp.zeros((DH, DH), F32)
    enter_gr = jnp.zeros((DH, DH), F32)
    for d, ref in ((1, c1), (2, c2), (3, c3)):
        earlier = info[X] >= d
        enter_kv = enter_kv + jnp.where(earlier, ref[...], 0.0)
        enter_gr = enter_gr + jnp.where(earlier, 0.0, ref[...])
    for e, out in enumerate((o0, o1, o2, o3)):
        there = (info[Y] + e) % 4
        kv, gr = enter_kv, enter_gr
        for d, ref in enumerate((g0, g1, g2, g3)):
            here = (info[Y] + 4 - d) % 4
            kv = kv + jnp.where(here < there, ref[0], 0.0)
            gr = gr + jnp.where(here > there, ref[1], 0.0)
        out[0] = kv
        out[1] = gr


def intra_kernel(pair):
    def kernel(p_ref, g_ref, att_ref, dq_ref, dk_ref, dv_ref):
        rows = lax.broadcasted_iota(jnp.int32, (BLK, BLK), 0)
        cols = lax.broadcasted_iota(jnp.int32, (BLK, BLK), 1)
        causal = rows >= cols
        for i in range(2):
            h = 2 * pair + i
            to = slice(i * DH, i * DH + DH)
            q, k, v = (p_ref[:, head(kind, h)] for kind in range(3))
            g = g_ref[:, head(0, h)]
            scores = jnp.where(causal, dot(q, k, 1, 1), 0.0).astype(BF16)
            att_ref[:, to] = dot(scores, v, 1, 0)
            dv_ref[:, to] = dot(scores, g, 0, 0)
            grad_scores = jnp.where(causal, dot(g, v, 1, 1), 0.0).astype(BF16)
            dq_ref[:, to] = dot(grad_scores, k, 1, 0)
            dk_ref[:, to] = dot(grad_scores, q, 0, 0)

    return kernel


def turn_kernel(own_ref, other_ref, o_ref):
    for j in range(4):
        at = slice(j * 512, j * 512 + 512)
        o_ref[at, 0:512] = own_ref[:, at].T
        o_ref[at, 512:1024] = other_ref[:, at].T


def settle_kernel(info, m0, m1, m2, m3, own_ref, other_ref, o_ref):
    c = info[CORE].astype(F32)
    o_ref[...] = jnp.zeros(o_ref.shape, BF16)
    for j, ref in enumerate((m0, m1, m2, m3)):
        for h in range(NEAR):

            @pl.when((info[Y] + 4 - j) % 4 == h)
            def _():
                at = slice((h % 2) * DH, (h % 2) * DH + DH)
                o_ref[0, h // 2, 0, at, at] = (ref[0] + c * other_ref[h, 0]).astype(BF16)
                o_ref[0, h // 2, 1, at, at] = (ref[1] + (1.0 - c) * other_ref[h, 1]).astype(BF16)
                o_ref[1, h // 2, 0, at, at] = (ref[0] + (1.0 - c) * own_ref[h, 0]).astype(BF16)
                o_ref[1, h // 2, 1, at, at] = (ref[1] + c * own_ref[h, 1]).astype(BF16)


def pair_of(kind, pair):
    return slice(kind * HALF + pair * 256, kind * HALF + pair * 256 + 256)


def rows_of(block):
    return slice(block * BLK, block * BLK + BLK)


def query_kernel(info, st_ref, go_ref, gp_ref, d00, d01, d10, d11, xt_ref, dq_ref, o_ref):
    parts = ((d00, d01), (d10, d11))
    for block, g_ref in enumerate((go_ref, gp_ref)):
        for pair in range(2):
            at = pair_of(0, pair)
            far = dot(g_ref[:, at], st_ref[block, pair, 0], 1, 1)
            dq_ref[rows_of(block), at] = (parts[block][pair][...] + far).astype(BF16)
    partial_x_kernel(0)(info, xt_ref, dq_ref, o_ref)


def key_value_kernel(
    info, st_ref, po_ref, pp_ref, k00, k01, k10, k11, v00, v01, v10, v11, xt_ref, dq_ref, dk_ref, dv_ref, o_ref, wide_ref
):
    keys = ((k00, k01), (k10, k11))
    values = ((v00, v01), (v10, v11))
    for block, p_ref in enumerate((po_ref, pp_ref)):
        for pair in range(2):
            at = pair_of(0, pair)
            gr = st_ref[block, pair, 1]
            far = dot(p_ref[:, pair_of(2, pair)], gr, 1, 1)
            dk_ref[rows_of(block), at] = (keys[block][pair][...] + far).astype(BF16)
            far = dot(p_ref[:, pair_of(1, pair)], gr, 1, 0)
            dv_ref[rows_of(block), at] = (values[block][pair][...] + far).astype(BF16)
    partial_y_kernel(0)(info, xt_ref, dk_ref, o_ref)
    for kind, ref in enumerate((dq_ref, dk_ref, dv_ref)):
        wide_ref[kind] = ref[512:1024, :].astype(F32)


def attend_kernel(info, st_ref, po_ref, pp_ref, a00, a01, a10, a11, own_ref, other_ref):
    parts = ((a00, a01), (a10, a11))
    scale = scale_of(info[BASE])
    for block, p_ref in enumerate((po_ref, pp_ref)):
        for pair in range(2):
            at = pair_of(0, pair)
            total = parts[block][pair][...] + dot(p_ref[:, at], st_ref[block, pair, 0], 1, 0)
            if block == 0:
                for i in range(2):
                    to = slice(pair * 256 + i * DH, pair * 256 + i * DH + DH)
                    own_ref[:, to] = (total[:, i * DH : i * DH + DH] * scale).astype(BF16)
            else:
                other_ref[:, at] = total


def attended_kernel(info, own_ref, back_ref, o_ref):
    scale = scale_of(info[BASE])
    for c in range(2):

        @pl.when(info[CORE] == c)
        def _():
            o_ref[:, c * HALF : c * HALF + HALF] = own_ref[...]
            for h in range(NEAR):
                to = slice((1 - c) * HALF + h * DH, (1 - c) * HALF + h * DH + DH)
                o_ref[:, to] = (back_ref[:, head(0, h)] * scale).astype(BF16)


def put(info, o_ref, lead, row, col, value):
    c = info[CORE]
    for i in range(2):
        half = jnp.where(c == i, 1, 0)
        o_ref[(*lead, half)] = value[row + i * 64 : row + i * 64 + 64, col : col + 128]


def slot(info, axis, i):
    return info[SLOTS[axis] + i]


def partial_x_kernel(keep):
    def kernel(info, xt_ref, d_ref, o_ref):
        for g in range(2):
            at = pl.multiple_of(info[PICKS["x"] + 2 * keep + g] * 512, 512)
            total = dot(xt_ref[pl.ds(at, 512), :], d_ref[...], 1, 0)
            for y in range(4):
                for z in range(4):
                    lead = (g, slot(info, "y", y), slot(info, "z", z))
                    put(info, o_ref, lead, y * 128, z * 128, total)

    return kernel


def partial_y_kernel(keep):
    def kernel(info, xt_ref, d_ref, o_ref):
        for g in range(2):
            y = info[PICKS["y"] + 2 * keep + g]
            left = [xt_ref[pl.ds(pl.multiple_of(x * 512 + y * 128, 128), 128), :] for x in range(4)]
            total = dot(jnp.concatenate(left, 0), d_ref[...], 1, 0)
            for x in range(4):
                for z in range(4):
                    lead = (g, slot(info, "z", z), slot(info, "x", x))
                    put(info, o_ref, lead, x * 128, z * 128, total)

    return kernel


def partial_z_kernel(keep):
    def kernel(info, xt_ref, d_ref, o_ref):
        right = []
        for g in range(2):
            at = pl.multiple_of(info[PICKS["z"] + 2 * keep + g] * 128, 128)
            right.append(d_ref[:, pl.ds(at, 128)])
        right = jnp.concatenate(right, 1)
        for x in range(4):
            total = dot(xt_ref[x * 512 : x * 512 + 512, :], right, 1, 0)
            for g in range(2):
                for y in range(4):
                    lead = (g, slot(info, "x", x), slot(info, "y", y))
                    put(info, o_ref, lead, y * 128, g * 128, total)

    return kernel


def tokens_out_kernel(info, dq_ref, dk_ref, dv_ref, back_ref, wo_ref, w_ref, o_ref, d_ref, wp_ref, sems):
    def copy(j, kind):
        at = pl.multiple_of((2 * kind + 1 - info[CORE]) * HALF, HALF)
        rows = pl.ds(j * 512, 512)
        return pltpu.make_async_copy(
            w_ref.at[rows, pl.ds(at, HALF)],
            wp_ref.at[rows, pl.ds(kind * HALF, HALF)],
            sems.at[3 * j + kind],
        )

    for j in range(4):
        for kind in range(3):
            copy(j, kind).start()
    for kind, ref in enumerate((dq_ref, dk_ref, dv_ref)):
        at = slice(kind * HALF, kind * HALF + HALF)
        d_ref[0, :, at] = ref[0:512, :]
        d_ref[1, :, at] = back_ref[kind].astype(BF16)
    for j in range(4):
        at = slice(j * 512, j * 512 + 512)
        own = dot(d_ref[0], wo_ref[at, :], 1, 1)
        for kind in range(3):
            copy(j, kind).wait()
        o_ref[:, at] = (own + dot(d_ref[1], wp_ref[at, :], 1, 1)).astype(BF16)


def second_kernel(kept_ref, came_ref, o_ref):
    o_ref[...] = kept_ref[1] + came_ref[1]


def regroup_kernel(kept_ref, came_ref, more_ref, sent_ref, keep_ref):
    sent_ref[...] = kept_ref[0, 0:2] + came_ref[0, 0:2] + more_ref[0:2]
    keep_ref[...] = kept_ref[0, 2:4] + came_ref[0, 2:4] + more_ref[2:4]


def rows_out_kernel(*refs):
    to_ref, own_ref = refs[9], refs[10]
    for third in range(3):
        kept_ref, came_ref, more_ref = refs[3 * third : 3 * third + 3]
        total = (kept_ref[0] + came_ref[0] + more_ref[...]) * (1.0 / 256.0)
        to_ref[third] = total[0]
        own_ref[third] = total[1]


def both_kernel(own_ref, came_ref, o_ref):
    o_ref[0] = own_ref[...]
    o_ref[1] = came_ref[...]


def weight_kernel(info, *refs):
    o_ref = refs[8]
    for d in range(4):
        z = (info[Z] + 4 - d) % 4
        for which in range(2):
            core = jnp.where(info[CORE] == which, 0, 1)
            for third in range(3):
                first = third * 1024 + core * HALF + z * DH
                o_ref[:, pl.ds(pl.multiple_of(first, DH), DH)] = refs[2 * d + which][third]


def after(values, done):
    return lax.optimization_barrier((values, done))[0]


def body(tokens, w_qkv, cotangent):
    device = lax.axis_index("seq") * 4 + lax.axis_index("batch")
    info = lax.dynamic_index_in_dim(jnp.asarray(table()), device, 0, keepdims=False)
    own_x = tokens[0]
    square = (2, DH, DH)
    (own_wide,) = call("widen", widen_kernel, None, [own_x], [((BLK, D), F32)])
    other_wide = permute(own_wide, core_pairs())
    own_g, sent_g, w_own = call(
        "grad",
        grad_kernel,
        info,
        after([cotangent[0], w_qkv], own_wide),
        [((BLK, HALF), BF16), ((BLK, HALF), F32), ((D, 3 * HALF), BF16)],
        scratch=[pltpu.SemaphoreType.DMA((3,))],
        stay=(1,),
    )
    other_gw = permute(sent_g, core_pairs())
    (own_p,) = call("project", project_kernel, None, [own_x, w_own], [((BLK, 3 * HALF), BF16)])
    (own_st,) = call("states", states_kernel, None, [own_p, own_g], [((NEAR,) + square, F32)])
    quarter = ((BLK, 256), F32)

    def intra(pair, p, g):
        return call("intra", intra_kernel(pair), None, [p, g], [quarter] * 4)

    other_p, other_x = call(
        "project_wide",
        project_wide_kernel,
        None,
        [after(other_wide, own_st), w_own],
        [((BLK, 3 * HALF), BF16), ((BLK, D), BF16)],
    )
    other_g, other_st, *pay = call(
        "chip_states",
        chip_states_kernel,
        info,
        [other_p, other_gw, own_st],
        [((BLK, HALF), BF16), ((NEAR,) + square, F32)] + [(square, F32)] * 4,
        scratch=[pltpu.VMEM((NEAR,) + square, F32)],
    )
    got = [pay[0]] + [permute(pay[d], shift_pairs("y", d)) for d in range(1, 4)]
    own_parts = [intra(0, *after((own_p, own_g), pay))]
    other_parts = [intra(0, *after((other_p, other_g), own_parts))]
    got = after(got, other_parts)
    rows = call("row", row_kernel, info, got, [((DH, DH), F32)] * 3)
    came = [permute(rows[d - 1], shift_pairs("x", d)) for d in range(1, 4)]
    own_parts.append(intra(1, *after((own_p, own_g), rows)))
    came = after(came, own_parts[1])
    back = call("back", back_kernel, info, got + came, [(square, F32)] * 4)
    mine = [back[0]] + [permute(back[e], shift_pairs("y", e)) for e in range(1, 4)]
    other_parts.append(intra(1, *after((other_p, other_g), back)))
    (xt,) = call("turn", turn_kernel, None, after([own_x, other_x], back), [((D, 1024), BF16)])
    mine = after(mine, (other_parts[1], xt))
    (state,) = call(
        "settle", settle_kernel, info, mine + [own_st, other_st], [((2, 2, 2, 256, 256), BF16)]
    )
    parts = [[own_parts[0][i], own_parts[1][i], other_parts[0][i], other_parts[1][i]] for i in range(4)]
    tall = ((1024, HALF), BF16)
    group = ((2, 4, 4, 2, 64, 128), F32)
    dq, sent_x = call(
        "query", query_kernel, info, [state, own_g, other_g] + parts[1] + [xt], [tall, group]
    )
    came_x = permute(sent_x, halving_pairs("x", 0))
    dk, dv, sent_y, wide_d = call(
        "key_value",
        key_value_kernel,
        info,
        [state, own_p, other_p] + parts[2] + parts[3] + [xt, dq],
        [tall, tall, group, ((3, BLK, HALF), F32)],
    )
    came_y = permute(sent_y, halving_pairs("y", 0))
    (sent_z,) = call("partial_z", partial_z_kernel(0), info, [xt, dv], [group])
    came_z = permute(sent_z, halving_pairs("z", 0))
    (kept_x,) = call("partial_x", partial_x_kernel(1), info, after([xt, dq], sent_z), [group])
    (kept_y,) = call("partial_y", partial_y_kernel(1), info, after([xt, dk], kept_x), [group])
    (kept_z,) = call("partial_z", partial_z_kernel(1), info, after([xt, dv], kept_y), [group])
    back_d = permute(wide_d, core_pairs())
    own_att, other_att = call(
        "attend",
        attend_kernel,
        info,
        [after(state, kept_z), own_p, other_p] + parts[0],
        [((BLK, HALF), BF16), ((BLK, HALF), F32)],
    )
    att_back = permute(other_att, core_pairs())
    args = after([dq, dk, dv, back_d], other_att)
    (token_grad,) = call(
        "tokens_out",
        tokens_out_kernel,
        info,
        args + [w_own, w_qkv],
        [((BLK, D), BF16)],
        scratch=[
            pltpu.VMEM((2, BLK, 3 * HALF), BF16),
            pltpu.VMEM((D, 3 * HALF), BF16),
            pltpu.SemaphoreType.DMA((12,)),
        ],
        stay=(5,),
    )
    thirds = [["xyz", kept_x, came_x], ["yzx", kept_y, came_y], ["zxy", kept_z, came_z]]
    last = token_grad
    for step in range(3):
        for third in thirds:
            axes, kept, came = third
            (last,) = call(
                "second", second_kernel, None, [kept, after(came, last)], [(kept.shape[1:], F32)]
            )
            third.append(permute(last, halving_pairs(axes[step], 1)))
        if step == 0:
            (attended,) = call(
                "attended",
                attended_kernel,
                info,
                [own_att, after(att_back, last)],
                [((BLK, 2 * HALF), BF16)],
            )
            last = attended
        if step < 2:
            for third in thirds:
                axes, kept, came, more = third
                outs = [((2,) + kept.shape[2:], F32)] * 2
                last, keep = call(
                    "regroup", regroup_kernel, None, [kept, came, after(more, last)], outs
                )
                third[1:] = [keep, permute(last, halving_pairs(axes[step + 1], 0))]
    to_other, own_w = call(
        "rows_out",
        rows_out_kernel,
        None,
        [part for third in thirds for part in third[1:]],
        [((3, 64, DH), F32)] * 2,
    )
    from_other = permute(to_other, core_pairs())
    along = [own_w, from_other]
    if SPREAD:
        for d in range(1, 4):
            along += [permute(own_w, shift_pairs("z", d)), permute(to_other, shift_pairs("z", d, True))]
    else:
        (pair,) = call("both", both_kernel, None, [own_w, from_other], [((2, 3, 64, DH), F32)])
        for d in range(1, 4):
            came = permute(pair, shift_pairs("z", d))
            along += [came[0], came[1]]
    (weight_grad,) = call("weight", weight_kernel, info, along, [((64, 3072), F32)])
    return attended[None], token_grad[None], weight_grad


def solution(mesh):
    return jax.shard_map(
        body,
        mesh=mesh,
        in_specs=(P("batch", "seq", None), P(), P("batch", "seq", None)),
        out_specs=(P("batch", "seq", None), P("batch", "seq", None), P("seq", None)),
        check_vma=False,
    )
```

```python
import jax
import jax.numpy as jnp
import numpy as np
from jax import lax
from jax.experimental import pallas as pl
from jax.experimental.pallas import tpu as pltpu
from jax.sharding import PartitionSpec as P

DH = 128
BLK = 512
D = 2048
HALF = 512
NEAR = 4
F32 = jnp.float32
BF16 = jnp.bfloat16
AXES = ("seq", "batch")
VMEM = 16 * 1024 * 1024
CORE, X, Y, Z, BASE, OTHER_BASE = range(6)
PICKS = dict(x=6, y=10, z=14)
SLOTS = dict(x=18, y=22, z=26)


def flat(x, y, c, z):
    return ((x * 4 + y) * 2 + c) * 4 + z


def every():
    for x in range(4):
        for y in range(4):
            for c in range(2):
                for z in range(4):
                    yield x, y, c, z


def partner(v, kind):
    return v ^ 1 if kind == 0 else 3 - v


def table():
    rows = np.zeros((128, 30), np.int32)
    for x, y, c, z in every():
        s = (x * 4 + y) * 2 + c
        row = [c, x, y, z, s * BLK, (s ^ 1) * BLK]
        for v in (x, y, z):
            w = partner(v, c)
            row += [w, partner(w, 1 - c), v, partner(v, 1 - c)]
        for first in (6, 10, 14):
            row += [row[first : first + 4].index(i) for i in range(4)]
        rows[flat(x, y, c, z)] = row
    return rows


def shift_pairs(axis, d):
    pairs = []
    for x, y, c, z in every():
        to = dict(x=x, y=y, z=z)
        to[axis] = (to[axis] + d) % 4
        pairs.append((flat(x, y, c, z), flat(to["x"], to["y"], c, to["z"])))
    return pairs


def core_pairs():
    return [(flat(x, y, c, z), flat(x, y, 1 - c, z)) for x, y, c, z in every()]


def halving_pairs(axes, step, swap=False):
    pairs = []
    for x, y, c, z in every():
        to = dict(x=x, y=y, z=z)
        for axis in axes:
            to[axis] = partner(to[axis], (c + step) % 2)
        pairs.append((flat(x, y, c, z), flat(to["x"], to["y"], c ^ int(swap), to["z"])))
    return pairs


def permute(value, pairs):
    return lax.ppermute(value, AXES, pairs)


def dot(a, b, contract_a, contract_b):
    return lax.dot_general(
        a, b, (((contract_a,), (contract_b,)), ((), ())), preferred_element_type=F32
    )


WHOLE = pl.BlockSpec(memory_space=pltpu.VMEM)
SCALARS = pl.BlockSpec(memory_space=pltpu.SMEM)
PLACED = pl.BlockSpec(memory_space=pltpu.MemorySpace.HBM)


def call(name, kernel, info, args, outs, scratch=(), stay=(), flops=1):
    specs = [PLACED if i in stay else WHOLE for i in range(len(args))]
    args = [
        pltpu.with_memory_space_constraint(a, pltpu.HBM) if i in stay else a for i, a in enumerate(args)
    ]
    if info is not None:
        specs = [SCALARS] + specs
        args = [info] + args
    return pl.pallas_call(
        kernel,
        out_shape=[jax.ShapeDtypeStruct(shape, kind) for shape, kind in outs],
        in_specs=specs,
        out_specs=[WHOLE] * len(outs),
        scratch_shapes=list(scratch),
        compiler_params=pltpu.CompilerParams(vmem_limit_bytes=VMEM),
        cost_estimate=pl.CostEstimate(flops=flops, bytes_accessed=1, transcendentals=0),
        name=name,
    )(*args)


def scale_of(base):
    position = base + lax.broadcasted_iota(jnp.int32, (BLK, DH), 0)
    return DH ** (-0.5) / jnp.sqrt(position.astype(F32) + 1.0)


def widen_kernel(x_ref, o_ref):
    o_ref[...] = x_ref[...].astype(F32)


def grad_kernel(info, cot_ref, own_ref, sent_ref):
    scale = scale_of(info[BASE])
    for c in range(2):

        @pl.when(info[CORE] == c)
        def _():
            for h in range(NEAR):
                to = slice(h * DH, h * DH + DH)
                for first, ref in ((c * HALF, own_ref), ((1 - c) * HALF, sent_ref)):
                    at = slice(first + h * DH, first + h * DH + DH)
                    low = (cot_ref[:, at].astype(F32) * scale).astype(BF16)
                    ref[:, to] = low.astype(ref.dtype)


def project_far_kernel(info, x_ref, w_ref, p_ref, wo_ref, wp_ref, sems):
    def copy(far, j):
        core = 1 - info[CORE] if far else info[CORE]
        at = pl.multiple_of((2 * j + core) * HALF, HALF)
        return pltpu.make_async_copy(
            w_ref.at[:, pl.ds(at, HALF)],
            (wp_ref if far else wo_ref).at[:, pl.ds(j * HALF, HALF)],
            sems.at[3 * int(far) + j],
        )

    for far in (True, False):
        for j in range(3):
            copy(far, j).start()
    for j in range(3):
        at = slice(j * HALF, (j + 1) * HALF)
        copy(True, j).wait()
        p_ref[:, at] = dot(x_ref[...], wp_ref[:, at], 1, 0).astype(BF16).astype(F32)
    for j in range(3):
        copy(False, j).wait()


def project_kernel(x_ref, w_ref, p_ref):
    for j in range(3):
        at = slice(j * HALF, (j + 1) * HALF)
        p_ref[:, at] = dot(x_ref[...], w_ref[:, at], 1, 0).astype(BF16)


def head(kind, h):
    return slice(kind * HALF + h * DH, kind * HALF + h * DH + DH)


def states_kernel(p_ref, g_ref, st_ref):
    for h in range(NEAR):
        st_ref[h, 0] = dot(p_ref[:, head(1, h)], p_ref[:, head(2, h)], 0, 0)
        st_ref[h, 1] = dot(p_ref[:, head(0, h)], g_ref[:, head(0, h)], 0, 0)


def chip_states_kernel(info, pw_ref, gw_ref, own_ref, p_ref, low_ref, st_ref, o0, o1, o2, o3, sum_ref):
    p_ref[...] = pw_ref[...].astype(BF16)
    low_ref[...] = gw_ref[...].astype(BF16)
    for h in range(NEAR):
        kv = dot(p_ref[:, head(1, h)], p_ref[:, head(2, h)], 0, 0)
        gr = dot(p_ref[:, head(0, h)], low_ref[:, head(0, h)], 0, 0)
        st_ref[h, 0] = kv
        st_ref[h, 1] = gr
        sum_ref[h, 0] = kv + own_ref[h, 0]
        sum_ref[h, 1] = gr + own_ref[h, 1]
    for d, ref in enumerate((o0, o1, o2, o3)):
        ref[...] = sum_ref[(info[Y] + d) % 4]


def row_kernel(info, g0, g1, g2, g3, o1, o2, o3):
    kv = g0[0] + g1[0] + g2[0] + g3[0]
    gr = g0[1] + g1[1] + g2[1] + g3[1]
    for d, ref in ((1, o1), (2, o2), (3, o3)):
        ref[...] = jnp.where(info[X] + d < 4, kv, gr)


def back_kernel(info, g0, g1, g2, g3, c1, c2, c3, o0, o1, o2, o3):
    enter_kv = jnp.zeros((DH, DH), F32)
    enter_gr = jnp.zeros((DH, DH), F32)
    for d, ref in ((1, c1), (2, c2), (3, c3)):
        earlier = info[X] >= d
        enter_kv = enter_kv + jnp.where(earlier, ref[...], 0.0)
        enter_gr = enter_gr + jnp.where(earlier, 0.0, ref[...])
    for e, out in enumerate((o0, o1, o2, o3)):
        there = (info[Y] + e) % 4
        kv, gr = enter_kv, enter_gr
        for d, ref in enumerate((g0, g1, g2, g3)):
            here = (info[Y] + 4 - d) % 4
            kv = kv + jnp.where(here < there, ref[0], 0.0)
            gr = gr + jnp.where(here > there, ref[1], 0.0)
        out[0] = kv
        out[1] = gr


def intra_kernel(pair):
    def kernel(p_ref, g_ref, att_ref, dq_ref, dk_ref, dv_ref):
        rows = lax.broadcasted_iota(jnp.int32, (BLK, BLK), 0)
        cols = lax.broadcasted_iota(jnp.int32, (BLK, BLK), 1)
        causal = rows >= cols
        for i in range(2):
            h = 2 * pair + i
            to = slice(i * DH, i * DH + DH)
            q, k, v = (p_ref[:, head(kind, h)] for kind in range(3))
            g = g_ref[:, head(0, h)]
            scores = jnp.where(causal, dot(q, k, 1, 1), 0.0).astype(BF16)
            att_ref[:, to] = dot(scores, v, 1, 0)
            dv_ref[:, to] = dot(scores, g, 0, 0)
            grad_scores = jnp.where(causal, dot(g, v, 1, 1), 0.0).astype(BF16)
            dq_ref[:, to] = dot(grad_scores, k, 1, 0)
            dk_ref[:, to] = dot(grad_scores, q, 0, 0)

    return kernel


def turn_kernel(own_ref, wide_ref, o_ref):
    for j in range(4):
        at = slice(j * 512, j * 512 + 512)
        o_ref[at, 0:512] = own_ref[:, at].T
        o_ref[at, 512:1024] = wide_ref[:, at].astype(BF16).T


def settle_kernel(info, m0, m1, m2, m3, own_ref, other_ref, o_ref):
    c = info[CORE].astype(F32)
    o_ref[...] = jnp.zeros(o_ref.shape, BF16)
    for j, ref in enumerate((m0, m1, m2, m3)):
        for h in range(NEAR):

            @pl.when((info[Y] + 4 - j) % 4 == h)
            def _():
                at = slice((h % 2) * DH, (h % 2) * DH + DH)
                o_ref[0, h // 2, 0, at, at] = (ref[0] + c * other_ref[h, 0]).astype(BF16)
                o_ref[0, h // 2, 1, at, at] = (ref[1] + (1.0 - c) * other_ref[h, 1]).astype(BF16)
                o_ref[1, h // 2, 0, at, at] = (ref[0] + (1.0 - c) * own_ref[h, 0]).astype(BF16)
                o_ref[1, h // 2, 1, at, at] = (ref[1] + c * own_ref[h, 1]).astype(BF16)


def pair_of(kind, pair):
    return slice(kind * HALF + pair * 256, kind * HALF + pair * 256 + 256)


def rows_of(block):
    return slice(block * BLK, block * BLK + BLK)


def query_kernel(info, st_ref, go_ref, gp_ref, d00, d01, d10, d11, xt_ref, dq_ref, o_ref):
    parts = ((d00, d01), (d10, d11))
    for block, g_ref in enumerate((go_ref, gp_ref)):
        for pair in range(2):
            at = pair_of(0, pair)
            far = dot(g_ref[:, at], st_ref[block, pair, 0], 1, 1)
            dq_ref[rows_of(block), at] = (parts[block][pair][...] + far).astype(BF16)
    partial_x_kernel(0)(info, xt_ref, dq_ref, o_ref)


def key_value_kernel(
    st_ref, po_ref, pp_ref, k00, k01, k10, k11, v00, v01, v10, v11, dq_ref, dk_ref, dv_ref, wide_ref
):
    keys = ((k00, k01), (k10, k11))
    values = ((v00, v01), (v10, v11))
    for block, p_ref in enumerate((po_ref, pp_ref)):
        for pair in range(2):
            at = pair_of(0, pair)
            gr = st_ref[block, pair, 1]
            far = dot(p_ref[:, pair_of(2, pair)], gr, 1, 1)
            dk_ref[rows_of(block), at] = (keys[block][pair][...] + far).astype(BF16)
            far = dot(p_ref[:, pair_of(1, pair)], gr, 1, 0)
            dv_ref[rows_of(block), at] = (values[block][pair][...] + far).astype(BF16)
    for kind, ref in enumerate((dq_ref, dk_ref, dv_ref)):
        wide_ref[kind] = ref[512:1024, :].astype(F32)


def attend_kernel(info, st_ref, po_ref, pp_ref, a00, a01, a10, a11, own_ref, other_ref):
    parts = ((a00, a01), (a10, a11))
    scale = scale_of(info[BASE])
    for block, p_ref in enumerate((po_ref, pp_ref)):
        for pair in range(2):
            at = pair_of(0, pair)
            total = parts[block][pair][...] + dot(p_ref[:, at], st_ref[block, pair, 0], 1, 0)
            if block == 0:
                for i in range(2):
                    to = slice(pair * 256 + i * DH, pair * 256 + i * DH + DH)
                    own_ref[:, to] = (total[:, i * DH : i * DH + DH] * scale).astype(BF16)
            else:
                other_ref[:, at] = total


def attended_kernel(info, own_ref, back_ref, o_ref):
    scale = scale_of(info[BASE])
    for c in range(2):

        @pl.when(info[CORE] == c)
        def _():
            o_ref[:, c * HALF : c * HALF + HALF] = own_ref[...]
            for h in range(NEAR):
                to = slice((1 - c) * HALF + h * DH, (1 - c) * HALF + h * DH + DH)
                o_ref[:, to] = (back_ref[:, head(0, h)] * scale).astype(BF16)


def put(info, o_ref, lead, row, col, value):
    c = info[CORE]
    for i in range(2):
        half = jnp.where(c == i, 1, 0)
        o_ref[(*lead, half)] = value[row + i * 64 : row + i * 64 + 64, col : col + 128]


def slot(info, axis, i):
    return info[SLOTS[axis] + i]


def partial_x_kernel(keep):
    def kernel(info, xt_ref, d_ref, o_ref):
        for g in range(2):
            at = pl.multiple_of(info[PICKS["x"] + 2 * keep + g] * 512, 512)
            total = dot(xt_ref[pl.ds(at, 512), :], d_ref[...], 1, 0)
            for y in range(4):
                for z in range(4):
                    lead = (g, slot(info, "y", y), slot(info, "z", z))
                    put(info, o_ref, lead, y * 128, z * 128, total)

    return kernel


def partial_y_kernel(keep):
    def kernel(info, xt_ref, d_ref, o_ref):
        for g in range(2):
            y = info[PICKS["y"] + 2 * keep + g]
            left = [xt_ref[pl.ds(pl.multiple_of(x * 512 + y * 128, 128), 128), :] for x in range(4)]
            total = dot(jnp.concatenate(left, 0), d_ref[...], 1, 0)
            for x in range(4):
                for z in range(4):
                    lead = (g, slot(info, "z", z), slot(info, "x", x))
                    put(info, o_ref, lead, x * 128, z * 128, total)

    return kernel


def partial_z_kernel(keep):
    def kernel(info, xt_ref, d_ref, o_ref):
        right = []
        for g in range(2):
            at = pl.multiple_of(info[PICKS["z"] + 2 * keep + g] * 128, 128)
            right.append(d_ref[:, pl.ds(at, 128)])
        right = jnp.concatenate(right, 1)
        for x in range(4):
            total = dot(xt_ref[x * 512 : x * 512 + 512, :], right, 1, 0)
            for g in range(2):
                for y in range(4):
                    lead = (g, slot(info, "x", x), slot(info, "y", y))
                    put(info, o_ref, lead, y * 128, g * 128, total)

    return kernel


def tokens_out_kernel(info, dq_ref, dk_ref, dv_ref, back_ref, wo_ref, w_ref, o_ref, d_ref, wp_ref, sems):
    def copy(j, kind):
        at = pl.multiple_of((2 * kind + 1 - info[CORE]) * HALF, HALF)
        rows = pl.ds(j * 512, 512)
        return pltpu.make_async_copy(
            w_ref.at[rows, pl.ds(at, HALF)],
            wp_ref.at[rows, pl.ds(kind * HALF, HALF)],
            sems.at[3 * j + kind],
        )

    for j in range(4):
        for kind in range(3):
            copy(j, kind).start()
    for kind, ref in enumerate((dq_ref, dk_ref, dv_ref)):
        at = slice(kind * HALF, kind * HALF + HALF)
        d_ref[0, :, at] = ref[0:512, :]
        d_ref[1, :, at] = back_ref[kind].astype(BF16)
    for j in range(4):
        at = slice(j * 512, j * 512 + 512)
        own = dot(d_ref[0], wo_ref[at, :], 1, 1)
        for kind in range(3):
            copy(j, kind).wait()
        o_ref[:, at] = (own + dot(d_ref[1], wp_ref[at, :], 1, 1)).astype(BF16)


def second_kernel(kept_ref, came_ref, sent_ref, keep_ref):
    sent_ref[...] = kept_ref[:, 0:2] + came_ref[:, 0:2]
    keep_ref[...] = kept_ref[:, 2:4] + came_ref[:, 2:4]


def third_kernel(kept_ref, came_ref, sent_ref, keep_ref):
    sent_ref[...] = kept_ref[:, :, 0:2] + came_ref[:, :, 0:2]
    keep_ref[...] = kept_ref[:, :, 2:4] + came_ref[:, :, 2:4]


def merge_kernel(kc, cc, kb, cb, ka, ca, own_ref, x_ref, y_ref, both_ref):
    for ref, i, j in ((own_ref, 0, 0), (x_ref, 1, 0), (y_ref, 0, 1), (both_ref, 1, 1)):
        for g in range(2):
            ref[0, g] = ka[i, j, g] + ca[i, j, g]
            ref[1, g] = kb[j, g, i] + cb[j, g, i]
            ref[2, g] = kc[g, i, j] + cc[g, i, j]


def gathered_kernel(own_ref, x_ref, y_ref, both_ref, o_ref):
    o_ref[...] = own_ref[...] + x_ref[...] + y_ref[...] + both_ref[...]


def rows_out_kernel(sum_ref, came_ref, to_ref, own_ref):
    for third in range(3):
        for g in range(2):
            total = (sum_ref[third, g] + came_ref[third, 1 - g]) * (1.0 / 256.0)
            to_ref[third, g] = total[0]
            own_ref[third, g] = total[1]


def weight_kernel(info, own_ref, core_ref, z_ref, both_ref, o_ref):
    far, across = info[PICKS["z"]], info[PICKS["z"] + 1]
    near = info[PICKS["z"] + 3]
    mine, other = info[CORE], 1 - info[CORE]
    for ref, core, groups in (
        (own_ref, mine, (info[Z], near)),
        (core_ref, other, (info[Z], far)),
        (z_ref, mine, (far, across)),
        (both_ref, other, (near, across)),
    ):
        for g in range(2):
            for third in range(3):
                first = third * 1024 + core * HALF + groups[g] * DH
                o_ref[:, pl.ds(pl.multiple_of(first, DH), DH)] = ref[third, g]


def after(values, done):
    return lax.optimization_barrier((values, done))[0]


def body(tokens, w_qkv, cotangent):
    device = lax.axis_index("seq") * 4 + lax.axis_index("batch")
    info = lax.dynamic_index_in_dim(jnp.asarray(table()), device, 0, keepdims=False)
    own_x = tokens[0]
    square = (2, DH, DH)
    far_p, w_own = call(
        "project_far",
        project_far_kernel,
        info,
        [own_x, w_qkv],
        [((BLK, 3 * HALF), F32), ((D, 3 * HALF), BF16)],
        scratch=[pltpu.VMEM((D, 3 * HALF), BF16), pltpu.SemaphoreType.DMA((6,))],
        stay=(1,),
    )
    other_pw = permute(far_p, core_pairs())
    own_g, sent_g = call(
        "grad",
        grad_kernel,
        info,
        [after(cotangent[0], far_p)],
        [((BLK, HALF), BF16), ((BLK, HALF), F32)],
    )
    other_gw = permute(sent_g, core_pairs())
    (own_p,) = call(
        "project", project_kernel, None, [own_x, after(w_own, own_g)], [((BLK, 3 * HALF), BF16)]
    )
    (own_st,) = call("states", states_kernel, None, [own_p, own_g], [((NEAR,) + square, F32)])
    quarter = ((BLK, 256), F32)

    def intra(pair, p, g):
        return call("intra", intra_kernel(pair), None, [p, g], [quarter] * 4)

    other_p, other_g, other_st, *pay = call(
        "chip_states",
        chip_states_kernel,
        info,
        [other_pw, other_gw, own_st],
        [((BLK, 3 * HALF), BF16), ((BLK, HALF), BF16), ((NEAR,) + square, F32)] + [(square, F32)] * 4,
        scratch=[pltpu.VMEM((NEAR,) + square, F32)],
    )
    got = [pay[0]] + [permute(pay[d], shift_pairs("y", d)) for d in range(1, 4)]
    (own_wide,) = call("widen", widen_kernel, None, [after(own_x, pay)], [((BLK, D), F32)])
    other_wide = permute(own_wide, core_pairs())
    own_parts = [intra(0, *after((own_p, own_g), own_wide))]
    other_parts = [intra(0, *after((other_p, other_g), own_parts))]
    got = after(got, other_parts)
    rows = call("row", row_kernel, info, got, [((DH, DH), F32)] * 3)
    came = [permute(rows[d - 1], shift_pairs("x", d)) for d in range(1, 4)]
    own_parts.append(intra(1, *after((own_p, own_g), rows)))
    came = after(came, own_parts[1])
    back = call("back", back_kernel, info, got + came, [(square, F32)] * 4)
    mine = [back[0]] + [permute(back[e], shift_pairs("y", e)) for e in range(1, 4)]
    other_parts.append(intra(1, *after((other_p, other_g), back)))
    (xt,) = call("turn", turn_kernel, None, after([own_x, other_wide], back), [((D, 1024), BF16)])
    mine = after(mine, (other_parts[1], xt))
    (state,) = call(
        "settle", settle_kernel, info, mine + [own_st, other_st], [((2, 2, 2, 256, 256), BF16)]
    )
    parts = [[own_parts[0][i], own_parts[1][i], other_parts[0][i], other_parts[1][i]] for i in range(4)]
    tall = ((1024, HALF), BF16)
    group = ((2, 4, 4, 2, 64, 128), F32)
    dq, sent_x = call(
        "query", query_kernel, info, [state, own_g, other_g] + parts[1] + [xt], [tall, group]
    )
    came_x = permute(sent_x, halving_pairs("x", 0))
    dk, dv, wide_d = call(
        "key_value",
        key_value_kernel,
        None,
        [state, own_p, other_p] + parts[2] + parts[3] + [dq],
        [tall, tall, ((3, BLK, HALF), F32)],
    )
    back_d = permute(wide_d, core_pairs())
    (sent_y,) = call("partial_y", partial_y_kernel(0), info, [xt, dk], [group])
    came_y = permute(sent_y, halving_pairs("y", 0))
    (sent_z,) = call("partial_z", partial_z_kernel(0), info, [xt, after(dv, sent_y)], [group])
    came_z = permute(sent_z, halving_pairs("z", 0))
    (kept_x,) = call("partial_x", partial_x_kernel(1), info, after([xt, dq], sent_z), [group])
    (kept_y,) = call("partial_y", partial_y_kernel(1), info, after([xt, dk], kept_x), [group])
    (kept_z,) = call("partial_z", partial_z_kernel(1), info, after([xt, dv], kept_y), [group])
    own_att, other_att = call(
        "attend",
        attend_kernel,
        info,
        [after(state, kept_z), own_p, other_p] + parts[0],
        [((BLK, HALF), BF16), ((BLK, HALF), F32)],
    )
    att_back = permute(other_att, core_pairs())
    (token_grad,) = call(
        "tokens_out",
        tokens_out_kernel,
        info,
        after([dq, dk, dv, back_d], other_att) + [w_own, w_qkv],
        [((BLK, D), BF16)],
        scratch=[
            pltpu.VMEM((2, BLK, 3 * HALF), BF16),
            pltpu.VMEM((D, 3 * HALF), BF16),
            pltpu.SemaphoreType.DMA((12,)),
        ],
        stay=(5,),
    )
    thirds = [["xyz", kept_x, came_x], ["yzx", kept_y, came_y], ["zxy", kept_z, came_z]]
    last = token_grad
    for step, kernel, shape in ((1, second_kernel, (2, 2, 4)), (2, third_kernel, (2, 2, 2))):
        for third in thirds:
            axes, kept, came = third
            last, keep = call(
                "halve", kernel, None, [kept, after(came, last)], [(shape + (2, 64, DH), F32)] * 2
            )
            third[1:] = [keep, permute(last, halving_pairs(axes[step], 0))]
        if step == 1:
            (attended,) = call(
                "attended",
                attended_kernel,
                info,
                [own_att, after(att_back, last)],
                [((BLK, 2 * HALF), BF16)],
            )
            last = attended
    block = ((3, 2, 2, 64, DH), F32)
    mine_w, to_x, to_y, to_both = call(
        "merge", merge_kernel, None, [part for third in thirds[::-1] for part in third[1:]], [block] * 4
    )
    from_x = permute(to_x, halving_pairs("x", 1))
    from_y = permute(to_y, halving_pairs("y", 1))
    from_both = permute(to_both, halving_pairs("xy", 1))
    (total,) = call("gathered", gathered_kernel, None, [mine_w, from_x, from_y, from_both], [block])
    from_z = permute(total, halving_pairs("z", 1))
    to_other, own_w = call(
        "rows_out", rows_out_kernel, None, [total, from_z], [((3, 2, 64, DH), F32)] * 2
    )
    along = [
        own_w,
        permute(to_other, core_pairs()),
        permute(own_w, halving_pairs("z", 0)),
        permute(to_other, halving_pairs("z", 0, True)),
    ]
    (weight_grad,) = call("weight", weight_kernel, info, along, [((64, 3072), F32)])
    return attended[None], token_grad[None], weight_grad


def solution(mesh):
    return jax.shard_map(
        body,
        mesh=mesh,
        in_specs=(P("batch", "seq", None), P(), P("batch", "seq", None)),
        out_specs=(P("batch", "seq", None), P("batch", "seq", None), P("seq", None)),
        check_vma=False,
    )
```

```python
import jax
import jax.numpy as jnp
import numpy as np
from jax import lax
from jax.experimental import pallas as pl
from jax.experimental.pallas import tpu as pltpu
from jax.sharding import PartitionSpec as P

DH = 128
BLK = 512
D = 2048
HALF = 512
NEAR = 4
F32 = jnp.float32
BF16 = jnp.bfloat16
AXES = ("seq", "batch")
VMEM = 8 * 1024 * 1024
VMEM_WEIGHTS = 20 * 1024 * 1024
CORE, X, Y, Z, BASE, OTHER_BASE = range(6)
PICKS = dict(x=6, y=10, z=14)
SLOTS = dict(x=18, y=22, z=26)


def flat(x, y, c, z):
    return ((x * 4 + y) * 2 + c) * 4 + z


def every():
    for x in range(4):
        for y in range(4):
            for c in range(2):
                for z in range(4):
                    yield x, y, c, z


def partner(v, kind):
    return v ^ 1 if kind == 0 else 3 - v


def table():
    rows = np.zeros((128, 30), np.int32)
    for x, y, c, z in every():
        s = (x * 4 + y) * 2 + c
        row = [c, x, y, z, s * BLK, (s ^ 1) * BLK]
        for v in (x, y, z):
            w = partner(v, c)
            row += [w, partner(w, 1 - c), v, partner(v, 1 - c)]
        for first in (6, 10, 14):
            row += [row[first : first + 4].index(i) for i in range(4)]
        rows[flat(x, y, c, z)] = row
    return rows


def shift_pairs(axis, d):
    pairs = []
    for x, y, c, z in every():
        to = dict(x=x, y=y, z=z)
        to[axis] = (to[axis] + d) % 4
        pairs.append((flat(x, y, c, z), flat(to["x"], to["y"], c, to["z"])))
    return pairs


def core_pairs():
    return [(flat(x, y, c, z), flat(x, y, 1 - c, z)) for x, y, c, z in every()]


def halving_pairs(axes, step, swap=False):
    pairs = []
    for x, y, c, z in every():
        to = dict(x=x, y=y, z=z)
        for axis in axes:
            to[axis] = partner(to[axis], (c + step) % 2)
        pairs.append((flat(x, y, c, z), flat(to["x"], to["y"], c ^ int(swap), to["z"])))
    return pairs


def permute(value, pairs):
    return lax.ppermute(value, AXES, pairs)


def dot(a, b, contract_a, contract_b):
    return lax.dot_general(
        a, b, (((contract_a,), (contract_b,)), ((), ())), preferred_element_type=F32
    )


WHOLE = pl.BlockSpec(memory_space=pltpu.VMEM)
SCALARS = pl.BlockSpec(memory_space=pltpu.SMEM)
PLACED = pl.BlockSpec(memory_space=pltpu.MemorySpace.HBM)


def call(name, kernel, info, args, outs, scratch=(), stay=(), flops=1):
    specs = [PLACED if i in stay else WHOLE for i in range(len(args))]
    args = [
        pltpu.with_memory_space_constraint(a, pltpu.HBM) if i in stay else a for i, a in enumerate(args)
    ]
    if info is not None:
        specs = [SCALARS] + specs
        args = [info] + args
    return pl.pallas_call(
        kernel,
        out_shape=[jax.ShapeDtypeStruct(shape, kind) for shape, kind in outs],
        in_specs=specs,
        out_specs=[WHOLE] * len(outs),
        scratch_shapes=list(scratch),
        compiler_params=pltpu.CompilerParams(vmem_limit_bytes=VMEM_WEIGHTS if stay else VMEM),
        cost_estimate=pl.CostEstimate(flops=flops, bytes_accessed=1, transcendentals=0),
        name=name,
    )(*args)


def scale_of(base):
    position = base + lax.broadcasted_iota(jnp.int32, (BLK, DH), 0)
    return DH ** (-0.5) / jnp.sqrt(position.astype(F32) + 1.0)


def widen_kernel(x_ref, o_ref):
    o_ref[...] = x_ref[...].astype(F32)


def grad_kernel(info, cot_ref, own_ref, sent_ref):
    scale = scale_of(info[BASE])
    for c in range(2):

        @pl.when(info[CORE] == c)
        def _():
            for h in range(NEAR):
                to = slice(h * DH, h * DH + DH)
                for first, ref in ((c * HALF, own_ref), ((1 - c) * HALF, sent_ref)):
                    at = slice(first + h * DH, first + h * DH + DH)
                    low = (cot_ref[:, at].astype(F32) * scale).astype(BF16)
                    ref[:, to] = low.astype(ref.dtype)


def project_far_kernel(info, x_ref, w_ref, p_ref, wo_ref, wp_ref, sems):
    def copy(far, j):
        core = 1 - info[CORE] if far else info[CORE]
        at = pl.multiple_of((2 * j + core) * HALF, HALF)
        return pltpu.make_async_copy(
            w_ref.at[:, pl.ds(at, HALF)],
            (wp_ref if far else wo_ref).at[:, pl.ds(j * HALF, HALF)],
            sems.at[3 * int(far) + j],
        )

    for far in (True, False):
        for j in range(3):
            copy(far, j).start()
    for j in range(3):
        at = slice(j * HALF, (j + 1) * HALF)
        copy(True, j).wait()
        p_ref[:, at] = dot(x_ref[...], wp_ref[:, at], 1, 0).astype(BF16).astype(F32)
    for j in range(3):
        copy(False, j).wait()


def project_kernel(x_ref, w_ref, p_ref):
    for j in range(3):
        at = slice(j * HALF, (j + 1) * HALF)
        p_ref[:, at] = dot(x_ref[...], w_ref[:, at], 1, 0).astype(BF16)


def head(kind, h):
    return slice(kind * HALF + h * DH, kind * HALF + h * DH + DH)


def states_kernel(p_ref, g_ref, st_ref):
    for h in range(NEAR):
        st_ref[h, 0] = dot(p_ref[:, head(1, h)], p_ref[:, head(2, h)], 0, 0)
        st_ref[h, 1] = dot(p_ref[:, head(0, h)], g_ref[:, head(0, h)], 0, 0)


def chip_states_kernel(info, pw_ref, gw_ref, own_ref, p_ref, low_ref, st_ref, o0, o1, o2, o3, sum_ref):
    p_ref[...] = pw_ref[...].astype(BF16)
    low_ref[...] = gw_ref[...].astype(BF16)
    for h in range(NEAR):
        kv = dot(p_ref[:, head(1, h)], p_ref[:, head(2, h)], 0, 0)
        gr = dot(p_ref[:, head(0, h)], low_ref[:, head(0, h)], 0, 0)
        st_ref[h, 0] = kv
        st_ref[h, 1] = gr
        sum_ref[h, 0] = kv + own_ref[h, 0]
        sum_ref[h, 1] = gr + own_ref[h, 1]
    for d, ref in enumerate((o0, o1, o2, o3)):
        ref[...] = sum_ref[(info[Y] + d) % 4]


def row_kernel(info, g0, g1, g2, g3, o1, o2, o3):
    kv = g0[0] + g1[0] + g2[0] + g3[0]
    gr = g0[1] + g1[1] + g2[1] + g3[1]
    for d, ref in ((1, o1), (2, o2), (3, o3)):
        ref[...] = jnp.where(info[X] + d < 4, kv, gr)


def back_kernel(info, g0, g1, g2, g3, c1, c2, c3, o0, o1, o2, o3):
    enter_kv = jnp.zeros((DH, DH), F32)
    enter_gr = jnp.zeros((DH, DH), F32)
    for d, ref in ((1, c1), (2, c2), (3, c3)):
        earlier = info[X] >= d
        enter_kv = enter_kv + jnp.where(earlier, ref[...], 0.0)
        enter_gr = enter_gr + jnp.where(earlier, 0.0, ref[...])
    for e, out in enumerate((o0, o1, o2, o3)):
        there = (info[Y] + e) % 4
        kv, gr = enter_kv, enter_gr
        for d, ref in enumerate((g0, g1, g2, g3)):
            here = (info[Y] + 4 - d) % 4
            kv = kv + jnp.where(here < there, ref[0], 0.0)
            gr = gr + jnp.where(here > there, ref[1], 0.0)
        out[0] = kv
        out[1] = gr


def intra_kernel(pair):
    def kernel(p_ref, g_ref, att_ref, dq_ref, dk_ref, dv_ref):
        rows = lax.broadcasted_iota(jnp.int32, (BLK, BLK), 0)
        cols = lax.broadcasted_iota(jnp.int32, (BLK, BLK), 1)
        causal = rows >= cols
        for i in range(2):
            h = 2 * pair + i
            to = slice(i * DH, i * DH + DH)
            q, k, v = (p_ref[:, head(kind, h)] for kind in range(3))
            g = g_ref[:, head(0, h)]
            scores = jnp.where(causal, dot(q, k, 1, 1), 0.0).astype(BF16)
            att_ref[:, to] = dot(scores, v, 1, 0)
            dv_ref[:, to] = dot(scores, g, 0, 0)
            grad_scores = jnp.where(causal, dot(g, v, 1, 1), 0.0).astype(BF16)
            dq_ref[:, to] = dot(grad_scores, k, 1, 0)
            dk_ref[:, to] = dot(grad_scores, q, 0, 0)

    return kernel


def turn_kernel(own_ref, wide_ref, o_ref):
    for j in range(4):
        at = slice(j * 512, j * 512 + 512)
        o_ref[at, 0:512] = own_ref[:, at].T
        o_ref[at, 512:1024] = wide_ref[:, at].astype(BF16).T


def settle_kernel(info, m0, m1, m2, m3, own_ref, other_ref, o_ref):
    c = info[CORE].astype(F32)
    o_ref[...] = jnp.zeros(o_ref.shape, BF16)
    for j, ref in enumerate((m0, m1, m2, m3)):
        for h in range(NEAR):

            @pl.when((info[Y] + 4 - j) % 4 == h)
            def _():
                at = slice((h % 2) * DH, (h % 2) * DH + DH)
                o_ref[0, h // 2, 0, at, at] = (ref[0] + c * other_ref[h, 0]).astype(BF16)
                o_ref[0, h // 2, 1, at, at] = (ref[1] + (1.0 - c) * other_ref[h, 1]).astype(BF16)
                o_ref[1, h // 2, 0, at, at] = (ref[0] + (1.0 - c) * own_ref[h, 0]).astype(BF16)
                o_ref[1, h // 2, 1, at, at] = (ref[1] + c * own_ref[h, 1]).astype(BF16)


def pair_of(kind, pair):
    return slice(kind * HALF + pair * 256, kind * HALF + pair * 256 + 256)


def rows_of(block):
    return slice(block * BLK, block * BLK + BLK)


def query_kernel(info, st_ref, go_ref, gp_ref, d00, d01, d10, d11, xt_ref, dq_ref, o_ref):
    parts = ((d00, d01), (d10, d11))
    for block, g_ref in enumerate((go_ref, gp_ref)):
        for pair in range(2):
            at = pair_of(0, pair)
            far = dot(g_ref[:, at], st_ref[block, pair, 0], 1, 1)
            dq_ref[rows_of(block), at] = (parts[block][pair][...] + far).astype(BF16)
    partial_x_kernel(0)(info, xt_ref, dq_ref, o_ref)


def key_value_kernel(
    st_ref, po_ref, pp_ref, k00, k01, k10, k11, v00, v01, v10, v11, dq_ref, dk_ref, dv_ref, wide_ref
):
    keys = ((k00, k01), (k10, k11))
    values = ((v00, v01), (v10, v11))
    for block, p_ref in enumerate((po_ref, pp_ref)):
        for pair in range(2):
            at = pair_of(0, pair)
            gr = st_ref[block, pair, 1]
            far = dot(p_ref[:, pair_of(2, pair)], gr, 1, 1)
            dk_ref[rows_of(block), at] = (keys[block][pair][...] + far).astype(BF16)
            far = dot(p_ref[:, pair_of(1, pair)], gr, 1, 0)
            dv_ref[rows_of(block), at] = (values[block][pair][...] + far).astype(BF16)
    for kind, ref in enumerate((dq_ref, dk_ref, dv_ref)):
        wide_ref[kind] = ref[512:1024, :].astype(F32)


def attend_kernel(info, st_ref, po_ref, pp_ref, a00, a01, a10, a11, own_ref, other_ref):
    parts = ((a00, a01), (a10, a11))
    scale = scale_of(info[BASE])
    for block, p_ref in enumerate((po_ref, pp_ref)):
        for pair in range(2):
            at = pair_of(0, pair)
            total = parts[block][pair][...] + dot(p_ref[:, at], st_ref[block, pair, 0], 1, 0)
            if block == 0:
                for i in range(2):
                    to = slice(pair * 256 + i * DH, pair * 256 + i * DH + DH)
                    own_ref[:, to] = (total[:, i * DH : i * DH + DH] * scale).astype(BF16)
            else:
                other_ref[:, at] = total


def attended_kernel(info, own_ref, back_ref, o_ref):
    scale = scale_of(info[BASE])
    for c in range(2):

        @pl.when(info[CORE] == c)
        def _():
            o_ref[:, c * HALF : c * HALF + HALF] = own_ref[...]
            for h in range(NEAR):
                to = slice((1 - c) * HALF + h * DH, (1 - c) * HALF + h * DH + DH)
                o_ref[:, to] = (back_ref[:, head(0, h)] * scale).astype(BF16)


def put(info, o_ref, lead, row, col, value):
    c = info[CORE]
    for i in range(2):
        half = jnp.where(c == i, 1, 0)
        o_ref[(*lead, half)] = value[row + i * 64 : row + i * 64 + 64, col : col + 128]


def slot(info, axis, i):
    return info[SLOTS[axis] + i]


def partial_x_kernel(keep):
    def kernel(info, xt_ref, d_ref, o_ref):
        for g in range(2):
            at = pl.multiple_of(info[PICKS["x"] + 2 * keep + g] * 512, 512)
            total = dot(xt_ref[pl.ds(at, 512), :], d_ref[...], 1, 0)
            for y in range(4):
                for z in range(4):
                    lead = (g, slot(info, "y", y), slot(info, "z", z))
                    put(info, o_ref, lead, y * 128, z * 128, total)

    return kernel


def partial_y_kernel(keep):
    def kernel(info, xt_ref, d_ref, o_ref):
        for g in range(2):
            y = info[PICKS["y"] + 2 * keep + g]
            left = [xt_ref[pl.ds(pl.multiple_of(x * 512 + y * 128, 128), 128), :] for x in range(4)]
            total = dot(jnp.concatenate(left, 0), d_ref[...], 1, 0)
            for x in range(4):
                for z in range(4):
                    lead = (g, slot(info, "z", z), slot(info, "x", x))
                    put(info, o_ref, lead, x * 128, z * 128, total)

    return kernel


def partial_z_kernel(keep):
    def kernel(info, xt_ref, d_ref, o_ref):
        right = []
        for g in range(2):
            at = pl.multiple_of(info[PICKS["z"] + 2 * keep + g] * 128, 128)
            right.append(d_ref[:, pl.ds(at, 128)])
        right = jnp.concatenate(right, 1)
        for x in range(4):
            total = dot(xt_ref[x * 512 : x * 512 + 512, :], right, 1, 0)
            for g in range(2):
                for y in range(4):
                    lead = (g, slot(info, "x", x), slot(info, "y", y))
                    put(info, o_ref, lead, y * 128, g * 128, total)

    return kernel


def tokens_out_kernel(info, dq_ref, dk_ref, dv_ref, back_ref, wo_ref, w_ref, o_ref, d_ref, wp_ref, sems):
    def copy(j, kind):
        at = pl.multiple_of((2 * kind + 1 - info[CORE]) * HALF, HALF)
        rows = pl.ds(j * 512, 512)
        return pltpu.make_async_copy(
            w_ref.at[rows, pl.ds(at, HALF)],
            wp_ref.at[rows, pl.ds(kind * HALF, HALF)],
            sems.at[3 * j + kind],
        )

    for j in range(4):
        for kind in range(3):
            copy(j, kind).start()
    for kind, ref in enumerate((dq_ref, dk_ref, dv_ref)):
        at = slice(kind * HALF, kind * HALF + HALF)
        d_ref[0, :, at] = ref[0:512, :]
        d_ref[1, :, at] = back_ref[kind].astype(BF16)
    for j in range(4):
        at = slice(j * 512, j * 512 + 512)
        own = dot(d_ref[0], wo_ref[at, :], 1, 1)
        for kind in range(3):
            copy(j, kind).wait()
        o_ref[:, at] = (own + dot(d_ref[1], wp_ref[at, :], 1, 1)).astype(BF16)


def second_kernel(kept_ref, came_ref, sent_ref, keep_ref):
    sent_ref[...] = kept_ref[:, 0:2] + came_ref[:, 0:2]
    keep_ref[...] = kept_ref[:, 2:4] + came_ref[:, 2:4]


def third_kernel(kept_ref, came_ref, sent_ref, keep_ref):
    sent_ref[...] = kept_ref[:, :, 0:2] + came_ref[:, :, 0:2]
    keep_ref[...] = kept_ref[:, :, 2:4] + came_ref[:, :, 2:4]


def sum_kernel(kept_ref, came_ref, o_ref):
    o_ref[...] = kept_ref[...] + came_ref[...]


def merge_kernel(a, b, kc, cc, own_ref, x_ref, y_ref, both_ref):
    for ref, i, j in ((own_ref, 0, 0), (x_ref, 1, 0), (y_ref, 0, 1), (both_ref, 1, 1)):
        for g in range(2):
            ref[0, g] = a[i, j, g]
            ref[1, g] = b[j, g, i]
            ref[2, g] = kc[g, i, j] + cc[g, i, j]


def gathered_kernel(own_ref, x_ref, y_ref, both_ref, o_ref):
    o_ref[...] = own_ref[...] + x_ref[...] + y_ref[...] + both_ref[...]


def rows_out_kernel(sum_ref, came_ref, to_ref, own_ref):
    for third in range(3):
        for g in range(2):
            total = (sum_ref[third, g] + came_ref[third, 1 - g]) * (1.0 / 256.0)
            to_ref[third, g] = total[0]
            own_ref[third, g] = total[1]


def weight_kernel(info, own_ref, core_ref, z_ref, both_ref, o_ref):
    far, across = info[PICKS["z"]], info[PICKS["z"] + 1]
    near = info[PICKS["z"] + 3]
    mine, other = info[CORE], 1 - info[CORE]
    for ref, core, groups in (
        (own_ref, mine, (info[Z], near)),
        (core_ref, other, (info[Z], far)),
        (z_ref, mine, (far, across)),
        (both_ref, other, (near, across)),
    ):
        for g in range(2):
            for third in range(3):
                first = third * 1024 + core * HALF + groups[g] * DH
                o_ref[:, pl.ds(pl.multiple_of(first, DH), DH)] = ref[third, g]


def after(values, done):
    return lax.optimization_barrier((values, done))[0]


def body(tokens, w_qkv, cotangent):
    device = lax.axis_index("seq") * 4 + lax.axis_index("batch")
    info = lax.dynamic_index_in_dim(jnp.asarray(table()), device, 0, keepdims=False)
    own_x = tokens[0]
    square = (2, DH, DH)
    far_p, w_own = call(
        "project_far",
        project_far_kernel,
        info,
        [own_x, w_qkv],
        [((BLK, 3 * HALF), F32), ((D, 3 * HALF), BF16)],
        scratch=[pltpu.VMEM((D, 3 * HALF), BF16), pltpu.SemaphoreType.DMA((6,))],
        stay=(1,),
    )
    other_pw = permute(far_p, core_pairs())
    own_g, sent_g = call(
        "grad",
        grad_kernel,
        info,
        [after(cotangent[0], far_p)],
        [((BLK, HALF), BF16), ((BLK, HALF), F32)],
    )
    other_gw = permute(sent_g, core_pairs())
    (own_p,) = call(
        "project", project_kernel, None, [own_x, after(w_own, own_g)], [((BLK, 3 * HALF), BF16)]
    )
    (own_st,) = call("states", states_kernel, None, [own_p, own_g], [((NEAR,) + square, F32)])
    quarter = ((BLK, 256), F32)

    def intra(pair, p, g):
        return call("intra", intra_kernel(pair), None, [p, g], [quarter] * 4)

    other_p, other_g, other_st, *pay = call(
        "chip_states",
        chip_states_kernel,
        info,
        [other_pw, other_gw, own_st],
        [((BLK, 3 * HALF), BF16), ((BLK, HALF), BF16), ((NEAR,) + square, F32)] + [(square, F32)] * 4,
        scratch=[pltpu.VMEM((NEAR,) + square, F32)],
    )
    got = [pay[0]] + [permute(pay[d], shift_pairs("y", d)) for d in range(1, 4)]
    (own_wide,) = call("widen", widen_kernel, None, [after(own_x, pay)], [((BLK, D), F32)])
    other_wide = permute(own_wide, core_pairs())
    own_parts = [intra(0, *after((own_p, own_g), own_wide))]
    other_parts = [intra(0, *after((other_p, other_g), own_parts))]
    got = after(got, other_parts)
    rows = call("row", row_kernel, info, got, [((DH, DH), F32)] * 3)
    came = [permute(rows[d - 1], shift_pairs("x", d)) for d in range(1, 4)]
    own_parts.append(intra(1, *after((own_p, own_g), rows)))
    came = after(came, own_parts[1])
    back = call("back", back_kernel, info, got + came, [(square, F32)] * 4)
    mine = [back[0]] + [permute(back[e], shift_pairs("y", e)) for e in range(1, 4)]
    other_parts.append(intra(1, *after((other_p, other_g), back)))
    (xt,) = call("turn", turn_kernel, None, after([own_x, other_wide], back), [((D, 1024), BF16)])
    mine = after(mine, (other_parts[1], xt))
    (state,) = call(
        "settle", settle_kernel, info, mine + [own_st, other_st], [((2, 2, 2, 256, 256), BF16)]
    )
    parts = [[own_parts[0][i], own_parts[1][i], other_parts[0][i], other_parts[1][i]] for i in range(4)]
    tall = ((1024, HALF), BF16)
    group = ((2, 4, 4, 2, 64, 128), F32)
    dq, sent_x = call(
        "query", query_kernel, info, [state, own_g, other_g] + parts[1] + [xt], [tall, group]
    )
    came_x = permute(sent_x, halving_pairs("x", 0))
    dk, dv, wide_d = call(
        "key_value",
        key_value_kernel,
        None,
        [state, own_p, other_p] + parts[2] + parts[3] + [dq],
        [tall, tall, ((3, BLK, HALF), F32)],
    )
    back_d = permute(wide_d, core_pairs())
    (sent_y,) = call("partial_y", partial_y_kernel(0), info, [xt, dk], [group])
    came_y = permute(sent_y, halving_pairs("y", 0))
    (sent_z,) = call("partial_z", partial_z_kernel(0), info, [xt, after(dv, sent_y)], [group])
    came_z = permute(sent_z, halving_pairs("z", 0))
    (kept_x,) = call("partial_x", partial_x_kernel(1), info, after([xt, dq], sent_z), [group])
    (kept_y,) = call("partial_y", partial_y_kernel(1), info, after([xt, dk], kept_x), [group])
    (kept_z,) = call("partial_z", partial_z_kernel(1), info, after([xt, dv], kept_y), [group])
    own_att, other_att = call(
        "attend",
        attend_kernel,
        info,
        [after(state, kept_z), own_p, other_p] + parts[0],
        [((BLK, HALF), BF16), ((BLK, HALF), F32)],
    )
    att_back = permute(other_att, core_pairs())
    (token_grad,) = call(
        "tokens_out",
        tokens_out_kernel,
        info,
        after([dq, dk, dv, back_d], other_att) + [w_own, w_qkv],
        [((BLK, D), BF16)],
        scratch=[
            pltpu.VMEM((2, BLK, 3 * HALF), BF16),
            pltpu.VMEM((D, 3 * HALF), BF16),
            pltpu.SemaphoreType.DMA((12,)),
        ],
        stay=(5,),
    )
    thirds = [["xyz", kept_x, came_x], ["yzx", kept_y, came_y], ["zxy", kept_z, came_z]]
    last = token_grad
    for step, kernel, shape in ((1, second_kernel, (2, 2, 4)), (2, third_kernel, (2, 2, 2))):
        for third in thirds:
            axes, kept, came = third
            last, keep = call(
                "halve", kernel, None, [kept, after(came, last)], [(shape + (2, 64, DH), F32)] * 2
            )
            third[1:] = [keep, permute(last, halving_pairs(axes[step], 0))]
        if step == 1:
            (attended,) = call(
                "attended",
                attended_kernel,
                info,
                [own_att, after(att_back, last)],
                [((BLK, 2 * HALF), BF16)],
            )
            last = attended
    block = ((3, 2, 2, 64, DH), F32)
    small = ((2, 2, 2, 2, 64, DH), F32)
    (sum_a,) = call("sum", sum_kernel, None, thirds[0][1:], [small])
    (sum_b,) = call("sum", sum_kernel, None, [thirds[1][1], after(thirds[1][2], sum_a)], [small])
    mine_w, to_x, to_y, to_both = call(
        "merge",
        merge_kernel,
        None,
        [sum_a, sum_b, thirds[2][1], after(thirds[2][2], sum_b)],
        [block] * 4,
    )
    from_x = permute(to_x, halving_pairs("x", 1))
    from_y = permute(to_y, halving_pairs("y", 1))
    from_both = permute(to_both, halving_pairs("xy", 1))
    (total,) = call("gathered", gathered_kernel, None, [mine_w, from_x, from_y, from_both], [block])
    from_z = permute(total, halving_pairs("z", 1))
    to_other, own_w = call(
        "rows_out", rows_out_kernel, None, [total, from_z], [((3, 2, 64, DH), F32)] * 2
    )
    along = [
        own_w,
        permute(to_other, core_pairs()),
        permute(own_w, halving_pairs("z", 0)),
        permute(to_other, halving_pairs("z", 0, True)),
    ]
    (weight_grad,) = call("weight", weight_kernel, info, along, [((64, 3072), F32)])
    return attended[None], token_grad[None], weight_grad


def solution(mesh):
    return jax.shard_map(
        body,
        mesh=mesh,
        in_specs=(P("batch", "seq", None), P(), P("batch", "seq", None)),
        out_specs=(P("batch", "seq", None), P("batch", "seq", None), P("seq", None)),
        check_vma=False,
    )
```

```python
import jax
import jax.numpy as jnp
import numpy as np
from jax import lax
from jax.experimental import pallas as pl
from jax.experimental.pallas import tpu as pltpu
from jax.sharding import PartitionSpec as P

DH = 128
BLK = 512
D = 2048
HALF = 512
NEAR = 4
F32 = jnp.float32
BF16 = jnp.bfloat16
AXES = ("seq", "batch")
VMEM = 8 * 1024 * 1024
VMEM_WEIGHTS = 20 * 1024 * 1024
CORE, X, Y, Z, BASE, OTHER_BASE = range(6)
PICKS = dict(x=6, y=10, z=14)
SLOTS = dict(x=18, y=22, z=26)


def flat(x, y, c, z):
    return ((x * 4 + y) * 2 + c) * 4 + z


def every():
    for x in range(4):
        for y in range(4):
            for c in range(2):
                for z in range(4):
                    yield x, y, c, z


def partner(v, kind):
    return v ^ 1 if kind == 0 else 3 - v


def table():
    rows = np.zeros((128, 30), np.int32)
    for x, y, c, z in every():
        s = (x * 4 + y) * 2 + c
        row = [c, x, y, z, s * BLK, (s ^ 1) * BLK]
        for v in (x, y, z):
            w = partner(v, c)
            row += [w, partner(w, 1 - c), v, partner(v, 1 - c)]
        for first in (6, 10, 14):
            row += [row[first : first + 4].index(i) for i in range(4)]
        rows[flat(x, y, c, z)] = row
    return rows


def shift_pairs(axis, d):
    pairs = []
    for x, y, c, z in every():
        to = dict(x=x, y=y, z=z)
        to[axis] = (to[axis] + d) % 4
        pairs.append((flat(x, y, c, z), flat(to["x"], to["y"], c, to["z"])))
    return pairs


def core_pairs():
    return [(flat(x, y, c, z), flat(x, y, 1 - c, z)) for x, y, c, z in every()]


def halving_pairs(axes, step, swap=False):
    pairs = []
    for x, y, c, z in every():
        to = dict(x=x, y=y, z=z)
        for axis in axes:
            to[axis] = partner(to[axis], (c + step) % 2)
        pairs.append((flat(x, y, c, z), flat(to["x"], to["y"], c ^ int(swap), to["z"])))
    return pairs


def permute(value, pairs):
    return lax.ppermute(value, AXES, pairs)


def dot(a, b, contract_a, contract_b):
    return lax.dot_general(
        a, b, (((contract_a,), (contract_b,)), ((), ())), preferred_element_type=F32
    )


WHOLE = pl.BlockSpec(memory_space=pltpu.VMEM)
SCALARS = pl.BlockSpec(memory_space=pltpu.SMEM)
PLACED = pl.BlockSpec(memory_space=pltpu.MemorySpace.HBM)


def call(name, kernel, info, args, outs, scratch=(), stay=(), flops=1):
    specs = [PLACED if i in stay else WHOLE for i in range(len(args))]
    args = [
        pltpu.with_memory_space_constraint(a, pltpu.HBM) if i in stay else a for i, a in enumerate(args)
    ]
    if info is not None:
        specs = [SCALARS] + specs
        args = [info] + args
    return pl.pallas_call(
        kernel,
        out_shape=[jax.ShapeDtypeStruct(shape, kind) for shape, kind in outs],
        in_specs=specs,
        out_specs=[WHOLE] * len(outs),
        scratch_shapes=list(scratch),
        compiler_params=pltpu.CompilerParams(vmem_limit_bytes=VMEM_WEIGHTS if stay else VMEM),
        cost_estimate=pl.CostEstimate(flops=flops, bytes_accessed=1, transcendentals=0),
        name=name,
    )(*args)


def scale_of(base):
    position = base + lax.broadcasted_iota(jnp.int32, (BLK, DH), 0)
    return DH ** (-0.5) / jnp.sqrt(position.astype(F32) + 1.0)


def widen_kernel(x_ref, o_ref):
    o_ref[...] = x_ref[...].astype(F32)


def grad_kernel(info, cot_ref, own_ref, sent_ref):
    scale = scale_of(info[BASE])
    for c in range(2):

        @pl.when(info[CORE] == c)
        def _():
            for h in range(NEAR):
                to = slice(h * DH, h * DH + DH)
                for first, ref in ((c * HALF, own_ref), ((1 - c) * HALF, sent_ref)):
                    at = slice(first + h * DH, first + h * DH + DH)
                    low = (cot_ref[:, at].astype(F32) * scale).astype(BF16)
                    ref[:, to] = low.astype(ref.dtype)


def project_far_kernel(info, x_hbm, w_ref, p_ref, wo_ref, x_ref, wp_ref, sems):
    def copy(far, j):
        core = 1 - info[CORE] if far else info[CORE]
        at = pl.multiple_of((2 * j + core) * HALF, HALF)
        return pltpu.make_async_copy(
            w_ref.at[:, pl.ds(at, HALF)],
            (wp_ref if far else wo_ref).at[:, pl.ds(j * HALF, HALF)],
            sems.at[3 * int(far) + j],
        )

    tokens = pltpu.make_async_copy(x_hbm, x_ref, sems.at[6])
    tokens.start()
    for j in range(3):
        copy(True, j).start()
    tokens.wait()
    for j in range(3):
        at = slice(j * HALF, (j + 1) * HALF)
        copy(True, j).wait()
        if j == 0:
            for k in range(3):
                copy(False, k).start()
        p_ref[:, at] = dot(x_ref[...], wp_ref[:, at], 1, 0).astype(BF16).astype(F32)
    for j in range(3):
        copy(False, j).wait()


def project_kernel(x_ref, w_ref, p_ref):
    for j in range(3):
        at = slice(j * HALF, (j + 1) * HALF)
        p_ref[:, at] = dot(x_ref[...], w_ref[:, at], 1, 0).astype(BF16)


def head(kind, h):
    return slice(kind * HALF + h * DH, kind * HALF + h * DH + DH)


def states_kernel(p_ref, g_ref, st_ref):
    for h in range(NEAR):
        st_ref[h, 0] = dot(p_ref[:, head(1, h)], p_ref[:, head(2, h)], 0, 0)
        st_ref[h, 1] = dot(p_ref[:, head(0, h)], g_ref[:, head(0, h)], 0, 0)


def chip_states_kernel(info, pw_ref, gw_ref, own_ref, p_ref, low_ref, st_ref, o0, o1, o2, o3, sum_ref):
    p_ref[...] = pw_ref[...].astype(BF16)
    low_ref[...] = gw_ref[...].astype(BF16)
    for h in range(NEAR):
        kv = dot(p_ref[:, head(1, h)], p_ref[:, head(2, h)], 0, 0)
        gr = dot(p_ref[:, head(0, h)], low_ref[:, head(0, h)], 0, 0)
        st_ref[h, 0] = kv
        st_ref[h, 1] = gr
        sum_ref[h, 0] = kv + own_ref[h, 0]
        sum_ref[h, 1] = gr + own_ref[h, 1]
    for d, ref in enumerate((o0, o1, o2, o3)):
        ref[...] = sum_ref[(info[Y] + d) % 4]


def row_kernel(info, g0, g1, g2, g3, o1, o2, o3):
    kv = g0[0] + g1[0] + g2[0] + g3[0]
    gr = g0[1] + g1[1] + g2[1] + g3[1]
    for d, ref in ((1, o1), (2, o2), (3, o3)):
        ref[...] = jnp.where(info[X] + d < 4, kv, gr)


def back_kernel(info, g0, g1, g2, g3, c1, c2, c3, o0, o1, o2, o3):
    enter_kv = jnp.zeros((DH, DH), F32)
    enter_gr = jnp.zeros((DH, DH), F32)
    for d, ref in ((1, c1), (2, c2), (3, c3)):
        earlier = info[X] >= d
        enter_kv = enter_kv + jnp.where(earlier, ref[...], 0.0)
        enter_gr = enter_gr + jnp.where(earlier, 0.0, ref[...])
    for e, out in enumerate((o0, o1, o2, o3)):
        there = (info[Y] + e) % 4
        kv, gr = enter_kv, enter_gr
        for d, ref in enumerate((g0, g1, g2, g3)):
            here = (info[Y] + 4 - d) % 4
            kv = kv + jnp.where(here < there, ref[0], 0.0)
            gr = gr + jnp.where(here > there, ref[1], 0.0)
        out[0] = kv
        out[1] = gr


def intra_kernel(pair):
    def kernel(p_ref, g_ref, att_ref, dq_ref, dk_ref, dv_ref):
        rows = lax.broadcasted_iota(jnp.int32, (BLK, BLK), 0)
        cols = lax.broadcasted_iota(jnp.int32, (BLK, BLK), 1)
        causal = rows >= cols
        for i in range(2):
            h = 2 * pair + i
            to = slice(i * DH, i * DH + DH)
            q, k, v = (p_ref[:, head(kind, h)] for kind in range(3))
            g = g_ref[:, head(0, h)]
            scores = jnp.where(causal, dot(q, k, 1, 1), 0.0).astype(BF16)
            att_ref[:, to] = dot(scores, v, 1, 0)
            dv_ref[:, to] = dot(scores, g, 0, 0)
            grad_scores = jnp.where(causal, dot(g, v, 1, 1), 0.0).astype(BF16)
            dq_ref[:, to] = dot(grad_scores, k, 1, 0)
            dk_ref[:, to] = dot(grad_scores, q, 0, 0)

    return kernel


def turn_kernel(own_ref, wide_ref, o_ref):
    for j in range(4):
        at = slice(j * 512, j * 512 + 512)
        o_ref[at, 0:512] = own_ref[:, at].T
        o_ref[at, 512:1024] = wide_ref[:, at].astype(BF16).T


def settle_kernel(info, m0, m1, m2, m3, own_ref, other_ref, o_ref):
    c = info[CORE].astype(F32)
    o_ref[...] = jnp.zeros(o_ref.shape, BF16)
    for j, ref in enumerate((m0, m1, m2, m3)):
        for h in range(NEAR):

            @pl.when((info[Y] + 4 - j) % 4 == h)
            def _():
                at = slice((h % 2) * DH, (h % 2) * DH + DH)
                o_ref[0, h // 2, 0, at, at] = (ref[0] + c * other_ref[h, 0]).astype(BF16)
                o_ref[0, h // 2, 1, at, at] = (ref[1] + (1.0 - c) * other_ref[h, 1]).astype(BF16)
                o_ref[1, h // 2, 0, at, at] = (ref[0] + (1.0 - c) * own_ref[h, 0]).astype(BF16)
                o_ref[1, h // 2, 1, at, at] = (ref[1] + c * own_ref[h, 1]).astype(BF16)


def pair_of(kind, pair):
    return slice(kind * HALF + pair * 256, kind * HALF + pair * 256 + 256)


def rows_of(block):
    return slice(block * BLK, block * BLK + BLK)


def query_kernel(info, st_ref, go_ref, gp_ref, d00, d01, d10, d11, xt_ref, dq_ref, o_ref):
    parts = ((d00, d01), (d10, d11))
    for block, g_ref in enumerate((go_ref, gp_ref)):
        for pair in range(2):
            at = pair_of(0, pair)
            far = dot(g_ref[:, at], st_ref[block, pair, 0], 1, 1)
            dq_ref[rows_of(block), at] = (parts[block][pair][...] + far).astype(BF16)
    partial_x_kernel(0)(info, xt_ref, dq_ref, o_ref)


def key_value_kernel(
    st_ref, po_ref, pp_ref, k00, k01, k10, k11, v00, v01, v10, v11, dq_ref, dk_ref, dv_ref, wide_ref
):
    keys = ((k00, k01), (k10, k11))
    values = ((v00, v01), (v10, v11))
    for block, p_ref in enumerate((po_ref, pp_ref)):
        for pair in range(2):
            at = pair_of(0, pair)
            gr = st_ref[block, pair, 1]
            far = dot(p_ref[:, pair_of(2, pair)], gr, 1, 1)
            dk_ref[rows_of(block), at] = (keys[block][pair][...] + far).astype(BF16)
            far = dot(p_ref[:, pair_of(1, pair)], gr, 1, 0)
            dv_ref[rows_of(block), at] = (values[block][pair][...] + far).astype(BF16)
    for kind, ref in enumerate((dq_ref, dk_ref, dv_ref)):
        wide_ref[kind] = ref[512:1024, :].astype(F32)


def attend_kernel(info, st_ref, po_ref, pp_ref, a00, a01, a10, a11, own_ref, other_ref):
    parts = ((a00, a01), (a10, a11))
    scale = scale_of(info[BASE])
    for block, p_ref in enumerate((po_ref, pp_ref)):
        for pair in range(2):
            at = pair_of(0, pair)
            total = parts[block][pair][...] + dot(p_ref[:, at], st_ref[block, pair, 0], 1, 0)
            if block == 0:
                for i in range(2):
                    to = slice(pair * 256 + i * DH, pair * 256 + i * DH + DH)
                    own_ref[:, to] = (total[:, i * DH : i * DH + DH] * scale).astype(BF16)
            else:
                other_ref[:, at] = total


def attended_kernel(info, own_ref, back_ref, o_ref):
    scale = scale_of(info[BASE])
    for c in range(2):

        @pl.when(info[CORE] == c)
        def _():
            o_ref[:, c * HALF : c * HALF + HALF] = own_ref[...]
            for h in range(NEAR):
                to = slice((1 - c) * HALF + h * DH, (1 - c) * HALF + h * DH + DH)
                o_ref[:, to] = (back_ref[:, head(0, h)] * scale).astype(BF16)


def put(info, o_ref, lead, row, col, value):
    c = info[CORE]
    for i in range(2):
        half = jnp.where(c == i, 1, 0)
        o_ref[(*lead, half)] = value[row + i * 64 : row + i * 64 + 64, col : col + 128]


def slot(info, axis, i):
    return info[SLOTS[axis] + i]


def partial_x_kernel(keep):
    def kernel(info, xt_ref, d_ref, o_ref):
        for g in range(2):
            at = pl.multiple_of(info[PICKS["x"] + 2 * keep + g] * 512, 512)
            total = dot(xt_ref[pl.ds(at, 512), :], d_ref[...], 1, 0)
            for y in range(4):
                for z in range(4):
                    lead = (g, slot(info, "y", y), slot(info, "z", z))
                    put(info, o_ref, lead, y * 128, z * 128, total)

    return kernel


def partial_y_kernel(keep):
    def kernel(info, xt_ref, d_ref, o_ref):
        for g in range(2):
            y = info[PICKS["y"] + 2 * keep + g]
            left = [xt_ref[pl.ds(pl.multiple_of(x * 512 + y * 128, 128), 128), :] for x in range(4)]
            total = dot(jnp.concatenate(left, 0), d_ref[...], 1, 0)
            for x in range(4):
                for z in range(4):
                    lead = (g, slot(info, "z", z), slot(info, "x", x))
                    put(info, o_ref, lead, x * 128, z * 128, total)

    return kernel


def partial_z_kernel(keep):
    def kernel(info, xt_ref, d_ref, o_ref):
        right = []
        for g in range(2):
            at = pl.multiple_of(info[PICKS["z"] + 2 * keep + g] * 128, 128)
            right.append(d_ref[:, pl.ds(at, 128)])
        right = jnp.concatenate(right, 1)
        for x in range(4):
            total = dot(xt_ref[x * 512 : x * 512 + 512, :], right, 1, 0)
            for g in range(2):
                for y in range(4):
                    lead = (g, slot(info, "x", x), slot(info, "y", y))
                    put(info, o_ref, lead, y * 128, g * 128, total)

    return kernel


def tokens_out_kernel(half):
    def kernel(info, dq_ref, dk_ref, dv_ref, back_ref, wo_ref, w_ref, *rest):
        first_ref = rest[0] if half else None
        o_ref, d_ref, wp_ref, sems = rest[half:]

        def copy(j, kind):
            at = pl.multiple_of((2 * kind + 1 - info[CORE]) * HALF, HALF)
            return pltpu.make_async_copy(
                w_ref.at[pl.ds(half * 1024 + j * 512, 512), pl.ds(at, HALF)],
                wp_ref.at[pl.ds(j * 512, 512), pl.ds(kind * HALF, HALF)],
                sems.at[3 * j + kind],
            )

        for j in range(2):
            for kind in range(3):
                copy(j, kind).start()
        for kind, ref in enumerate((dq_ref, dk_ref, dv_ref)):
            at = slice(kind * HALF, kind * HALF + HALF)
            d_ref[0, :, at] = ref[0:512, :]
            d_ref[1, :, at] = back_ref[kind].astype(BF16)
        if half:
            o_ref[:, 0:1024] = first_ref[...]
        for j in range(2):
            at = half * 1024 + j * 512
            own = dot(d_ref[0], wo_ref[at : at + 512, :], 1, 1)
            for kind in range(3):
                copy(j, kind).wait()
            far = dot(d_ref[1], wp_ref[j * 512 : j * 512 + 512, :], 1, 1)
            o_ref[:, at : at + 512] = (own + far).astype(BF16)

    return kernel


def second_kernel(kept_ref, came_ref, sent_ref, keep_ref):
    sent_ref[...] = kept_ref[:, 0:2] + came_ref[:, 0:2]
    keep_ref[...] = kept_ref[:, 2:4] + came_ref[:, 2:4]


def third_kernel(kept_ref, came_ref, sent_ref, keep_ref):
    sent_ref[...] = kept_ref[:, :, 0:2] + came_ref[:, :, 0:2]
    keep_ref[...] = kept_ref[:, :, 2:4] + came_ref[:, :, 2:4]


def sum_kernel(kept_ref, came_ref, o_ref):
    o_ref[...] = kept_ref[...] + came_ref[...]


def merge_kernel(a, b, kc, cc, own_ref, x_ref, y_ref, both_ref):
    for ref, i, j in ((own_ref, 0, 0), (x_ref, 1, 0), (y_ref, 0, 1), (both_ref, 1, 1)):
        for g in range(2):
            ref[0, g] = a[i, j, g]
            ref[1, g] = b[j, g, i]
            ref[2, g] = kc[g, i, j] + cc[g, i, j]


def gathered_kernel(own_ref, x_ref, y_ref, both_ref, o_ref):
    o_ref[...] = own_ref[...] + x_ref[...] + y_ref[...] + both_ref[...]


def rows_out_kernel(sum_ref, came_ref, to_ref, own_ref):
    for third in range(3):
        for g in range(2):
            total = (sum_ref[third, g] + came_ref[third, 1 - g]) * (1.0 / 256.0)
            to_ref[third, g] = total[0]
            own_ref[third, g] = total[1]


def weight_kernel(info, own_ref, core_ref, z_ref, both_ref, o_ref):
    far, across = info[PICKS["z"]], info[PICKS["z"] + 1]
    near = info[PICKS["z"] + 3]
    mine, other = info[CORE], 1 - info[CORE]
    for ref, core, groups in (
        (own_ref, mine, (info[Z], near)),
        (core_ref, other, (info[Z], far)),
        (z_ref, mine, (far, across)),
        (both_ref, other, (near, across)),
    ):
        for g in range(2):
            for third in range(3):
                first = third * 1024 + core * HALF + groups[g] * DH
                o_ref[:, pl.ds(pl.multiple_of(first, DH), DH)] = ref[third, g]


def after(values, done):
    return lax.optimization_barrier((values, done))[0]


def body(tokens, w_qkv, cotangent):
    device = lax.axis_index("seq") * 4 + lax.axis_index("batch")
    info = lax.dynamic_index_in_dim(jnp.asarray(table()), device, 0, keepdims=False)
    own_x = tokens[0]
    square = (2, DH, DH)
    far_p, w_own = call(
        "project_far",
        project_far_kernel,
        info,
        [own_x, w_qkv],
        [((BLK, 3 * HALF), F32), ((D, 3 * HALF), BF16)],
        scratch=[
            pltpu.VMEM((BLK, D), BF16),
            pltpu.VMEM((D, 3 * HALF), BF16),
            pltpu.SemaphoreType.DMA((7,)),
        ],
        stay=(0, 1),
    )
    other_pw = permute(far_p, core_pairs())
    own_g, sent_g = call(
        "grad",
        grad_kernel,
        info,
        [after(cotangent[0], far_p)],
        [((BLK, HALF), BF16), ((BLK, HALF), F32)],
    )
    other_gw = permute(sent_g, core_pairs())
    (own_p,) = call(
        "project", project_kernel, None, [own_x, after(w_own, own_g)], [((BLK, 3 * HALF), BF16)]
    )
    (own_st,) = call("states", states_kernel, None, [own_p, own_g], [((NEAR,) + square, F32)])
    quarter = ((BLK, 256), F32)

    def intra(pair, p, g):
        return call("intra", intra_kernel(pair), None, [p, g], [quarter] * 4)

    other_p, other_g, other_st, *pay = call(
        "chip_states",
        chip_states_kernel,
        info,
        [other_pw, other_gw, own_st],
        [((BLK, 3 * HALF), BF16), ((BLK, HALF), BF16), ((NEAR,) + square, F32)] + [(square, F32)] * 4,
        scratch=[pltpu.VMEM((NEAR,) + square, F32)],
    )
    got = [pay[0]] + [permute(pay[d], shift_pairs("y", d)) for d in range(1, 4)]
    (own_wide,) = call("widen", widen_kernel, None, [after(own_x, pay)], [((BLK, D), F32)])
    other_wide = permute(own_wide, core_pairs())
    own_parts = [intra(0, *after((own_p, own_g), own_wide))]
    other_parts = [intra(0, *after((other_p, other_g), own_parts))]
    got = after(got, other_parts)
    rows = call("row", row_kernel, info, got, [((DH, DH), F32)] * 3)
    came = [permute(rows[d - 1], shift_pairs("x", d)) for d in range(1, 4)]
    own_parts.append(intra(1, *after((own_p, own_g), rows)))
    came = after(came, own_parts[1])
    back = call("back", back_kernel, info, got + came, [(square, F32)] * 4)
    mine = [back[0]] + [permute(back[e], shift_pairs("y", e)) for e in range(1, 4)]
    other_parts.append(intra(1, *after((other_p, other_g), back)))
    (xt,) = call("turn", turn_kernel, None, after([own_x, other_wide], back), [((D, 1024), BF16)])
    mine = after(mine, (other_parts[1], xt))
    (state,) = call(
        "settle", settle_kernel, info, mine + [own_st, other_st], [((2, 2, 2, 256, 256), BF16)]
    )
    parts = [[own_parts[0][i], own_parts[1][i], other_parts[0][i], other_parts[1][i]] for i in range(4)]
    tall = ((1024, HALF), BF16)
    group = ((2, 4, 4, 2, 64, 128), F32)
    dq, sent_x = call(
        "query", query_kernel, info, [state, own_g, other_g] + parts[1] + [xt], [tall, group]
    )
    came_x = permute(sent_x, halving_pairs("x", 0))
    dk, dv, wide_d = call(
        "key_value",
        key_value_kernel,
        None,
        [state, own_p, other_p] + parts[2] + parts[3] + [dq],
        [tall, tall, ((3, BLK, HALF), F32)],
    )
    back_d = permute(wide_d, core_pairs())
    (sent_y,) = call("partial_y", partial_y_kernel(0), info, [xt, dk], [group])
    came_y = permute(sent_y, halving_pairs("y", 0))
    (sent_z,) = call("partial_z", partial_z_kernel(0), info, [xt, after(dv, sent_y)], [group])
    came_z = permute(sent_z, halving_pairs("z", 0))
    (kept_x,) = call("partial_x", partial_x_kernel(1), info, after([xt, dq], sent_z), [group])
    (kept_y,) = call("partial_y", partial_y_kernel(1), info, after([xt, dk], kept_x), [group])
    (kept_z,) = call("partial_z", partial_z_kernel(1), info, after([xt, dv], kept_y), [group])
    own_att, other_att = call(
        "attend",
        attend_kernel,
        info,
        [after(state, kept_z), own_p, other_p] + parts[0],
        [((BLK, HALF), BF16), ((BLK, HALF), F32)],
    )
    att_back = permute(other_att, core_pairs())
    low = [
        pltpu.VMEM((2, BLK, 3 * HALF), BF16),
        pltpu.VMEM((1024, 3 * HALF), BF16),
        pltpu.SemaphoreType.DMA((6,)),
    ]
    d_args = after([dq, dk, dv, back_d], other_att)
    (token_half,) = call(
        "tokens_out",
        tokens_out_kernel(0),
        info,
        d_args + [w_own, w_qkv],
        [((BLK, 1024), BF16)],
        scratch=low,
        stay=(5,),
    )
    thirds = [["xyz", kept_x, came_x], ["yzx", kept_y, came_y], ["zxy", kept_z, came_z]]
    last = token_half
    for step, kernel, shape in ((1, second_kernel, (2, 2, 4)), (2, third_kernel, (2, 2, 2))):
        for third in thirds:
            axes, kept, came = third
            last, keep = call(
                "halve", kernel, None, [kept, after(came, last)], [(shape + (2, 64, DH), F32)] * 2
            )
            third[1:] = [keep, permute(last, halving_pairs(axes[step], 0))]
        if step == 1:
            (token_grad,) = call(
                "tokens_out",
                tokens_out_kernel(1),
                info,
                after(d_args, last) + [w_own, w_qkv, token_half],
                [((BLK, D), BF16)],
                scratch=low,
                stay=(5,),
            )
            (attended,) = call(
                "attended",
                attended_kernel,
                info,
                [own_att, after(att_back, token_grad)],
                [((BLK, 2 * HALF), BF16)],
            )
            last = attended
    block = ((3, 2, 2, 64, DH), F32)
    small = ((2, 2, 2, 2, 64, DH), F32)
    (sum_a,) = call("sum", sum_kernel, None, thirds[0][1:], [small])
    (sum_b,) = call("sum", sum_kernel, None, [thirds[1][1], after(thirds[1][2], sum_a)], [small])
    mine_w, to_x, to_y, to_both = call(
        "merge",
        merge_kernel,
        None,
        [sum_a, sum_b, thirds[2][1], after(thirds[2][2], sum_b)],
        [block] * 4,
    )
    from_x = permute(to_x, halving_pairs("x", 1))
    from_y = permute(to_y, halving_pairs("y", 1))
    from_both = permute(to_both, halving_pairs("xy", 1))
    (total,) = call("gathered", gathered_kernel, None, [mine_w, from_x, from_y, from_both], [block])
    from_z = permute(total, halving_pairs("z", 1))
    to_other, own_w = call(
        "rows_out", rows_out_kernel, None, [total, from_z], [((3, 2, 64, DH), F32)] * 2
    )
    along = [
        own_w,
        permute(to_other, core_pairs()),
        permute(own_w, halving_pairs("z", 0)),
        permute(to_other, halving_pairs("z", 0, True)),
    ]
    (weight_grad,) = call("weight", weight_kernel, info, along, [((64, 3072), F32)])
    return attended[None], token_grad[None], weight_grad


def solution(mesh):
    return jax.shard_map(
        body,
        mesh=mesh,
        in_specs=(P("batch", "seq", None), P(), P("batch", "seq", None)),
        out_specs=(P("batch", "seq", None), P("batch", "seq", None), P("seq", None)),
        check_vma=False,
    )
```

```python
import jax
import jax.numpy as jnp
import numpy as np
from jax import lax
from jax.experimental import pallas as pl
from jax.experimental.pallas import tpu as pltpu
from jax.sharding import PartitionSpec as P

DH = 128
BLK = 512
D = 2048
HALF = 512
NEAR = 4
F32 = jnp.float32
BF16 = jnp.bfloat16
AXES = ("seq", "batch")
VMEM = 8 * 1024 * 1024
VMEM_WEIGHTS = 20 * 1024 * 1024
CORE, X, Y, Z, BASE, OTHER_BASE = range(6)
PICKS = dict(x=6, y=10, z=14)
SLOTS = dict(x=18, y=22, z=26)


def flat(x, y, c, z):
    return ((x * 4 + y) * 2 + c) * 4 + z


def every():
    for x in range(4):
        for y in range(4):
            for c in range(2):
                for z in range(4):
                    yield x, y, c, z


def partner(v, kind):
    return v ^ 1 if kind == 0 else 3 - v


def table():
    rows = np.zeros((128, 30), np.int32)
    for x, y, c, z in every():
        s = (x * 4 + y) * 2 + c
        row = [c, x, y, z, s * BLK, (s ^ 1) * BLK]
        for v in (x, y, z):
            w = partner(v, c)
            row += [w, partner(w, 1 - c), v, partner(v, 1 - c)]
        for first in (6, 10, 14):
            row += [row[first : first + 4].index(i) for i in range(4)]
        rows[flat(x, y, c, z)] = row
    return rows


def shift_pairs(axis, d):
    pairs = []
    for x, y, c, z in every():
        to = dict(x=x, y=y, z=z)
        to[axis] = (to[axis] + d) % 4
        pairs.append((flat(x, y, c, z), flat(to["x"], to["y"], c, to["z"])))
    return pairs


def core_pairs():
    return [(flat(x, y, c, z), flat(x, y, 1 - c, z)) for x, y, c, z in every()]


def halving_pairs(axes, step, swap=False):
    pairs = []
    for x, y, c, z in every():
        to = dict(x=x, y=y, z=z)
        for axis in axes:
            to[axis] = partner(to[axis], (c + step) % 2)
        pairs.append((flat(x, y, c, z), flat(to["x"], to["y"], c ^ int(swap), to["z"])))
    return pairs


def permute(value, pairs):
    return lax.ppermute(value, AXES, pairs)


def dot(a, b, contract_a, contract_b):
    return lax.dot_general(
        a, b, (((contract_a,), (contract_b,)), ((), ())), preferred_element_type=F32
    )


WHOLE = pl.BlockSpec(memory_space=pltpu.VMEM)
SCALARS = pl.BlockSpec(memory_space=pltpu.SMEM)
PLACED = pl.BlockSpec(memory_space=pltpu.MemorySpace.HBM)


def call(name, kernel, info, args, outs, scratch=(), stay=(), flops=1):
    specs = [PLACED if i in stay else WHOLE for i in range(len(args))]
    args = [
        pltpu.with_memory_space_constraint(a, pltpu.HBM) if i in stay else a for i, a in enumerate(args)
    ]
    if info is not None:
        specs = [SCALARS] + specs
        args = [info] + args
    return pl.pallas_call(
        kernel,
        out_shape=[jax.ShapeDtypeStruct(shape, kind) for shape, kind in outs],
        in_specs=specs,
        out_specs=[WHOLE] * len(outs),
        scratch_shapes=list(scratch),
        compiler_params=pltpu.CompilerParams(vmem_limit_bytes=VMEM_WEIGHTS if stay else VMEM),
        cost_estimate=pl.CostEstimate(flops=flops, bytes_accessed=1, transcendentals=0),
        name=name,
    )(*args)


def scale_of(base):
    position = base + lax.broadcasted_iota(jnp.int32, (BLK, DH), 0)
    return DH ** (-0.5) / jnp.sqrt(position.astype(F32) + 1.0)


def widen_kernel(x_ref, o_ref):
    o_ref[...] = x_ref[...].astype(F32)


def grad_kernel(info, cot_ref, own_ref, sent_ref):
    scale = scale_of(info[BASE])
    for c in range(2):

        @pl.when(info[CORE] == c)
        def _():
            for h in range(NEAR):
                to = slice(h * DH, h * DH + DH)
                for first, ref in ((c * HALF, own_ref), ((1 - c) * HALF, sent_ref)):
                    at = slice(first + h * DH, first + h * DH + DH)
                    low = (cot_ref[:, at].astype(F32) * scale).astype(BF16)
                    ref[:, to] = low.astype(ref.dtype)


def project_far_kernel(info, x_hbm, w_ref, p_ref, wo_ref, x_ref, wp_ref, sems):
    def copy(far, j):
        core = 1 - info[CORE] if far else info[CORE]
        at = pl.multiple_of((2 * j + core) * HALF, HALF)
        return pltpu.make_async_copy(
            w_ref.at[:, pl.ds(at, HALF)],
            (wp_ref if far else wo_ref).at[:, pl.ds(j * HALF, HALF)],
            sems.at[3 * int(far) + j],
        )

    tokens = pltpu.make_async_copy(x_hbm, x_ref, sems.at[6])
    tokens.start()
    for j in range(3):
        copy(True, j).start()
    tokens.wait()
    for j in range(3):
        at = slice(j * HALF, (j + 1) * HALF)
        copy(True, j).wait()
        if j == 0:
            for k in range(3):
                copy(False, k).start()
        p_ref[:, at] = dot(x_ref[...], wp_ref[:, at], 1, 0).astype(BF16).astype(F32)
    for j in range(3):
        copy(False, j).wait()


def project_kernel(x_ref, w_ref, p_ref):
    for j in range(3):
        at = slice(j * HALF, (j + 1) * HALF)
        p_ref[:, at] = dot(x_ref[...], w_ref[:, at], 1, 0).astype(BF16)


def head(kind, h):
    return slice(kind * HALF + h * DH, kind * HALF + h * DH + DH)


def states_kernel(p_ref, g_ref, st_ref):
    for h in range(NEAR):
        st_ref[h, 0] = dot(p_ref[:, head(1, h)], p_ref[:, head(2, h)], 0, 0)
        st_ref[h, 1] = dot(p_ref[:, head(0, h)], g_ref[:, head(0, h)], 0, 0)


def chip_states_kernel(info, pw_ref, gw_ref, own_ref, p_ref, low_ref, st_ref, o0, o1, o2, o3, sum_ref):
    p_ref[...] = pw_ref[...].astype(BF16)
    low_ref[...] = gw_ref[...].astype(BF16)
    for h in range(NEAR):
        kv = dot(p_ref[:, head(1, h)], p_ref[:, head(2, h)], 0, 0)
        gr = dot(p_ref[:, head(0, h)], low_ref[:, head(0, h)], 0, 0)
        st_ref[h, 0] = kv
        st_ref[h, 1] = gr
        sum_ref[h, 0] = kv + own_ref[h, 0]
        sum_ref[h, 1] = gr + own_ref[h, 1]
    for d, ref in enumerate((o0, o1, o2, o3)):
        ref[...] = sum_ref[(info[Y] + d) % 4]


def row_kernel(info, g0, g1, g2, g3, o1, o2, o3):
    kv = g0[0] + g1[0] + g2[0] + g3[0]
    gr = g0[1] + g1[1] + g2[1] + g3[1]
    for d, ref in ((1, o1), (2, o2), (3, o3)):
        ref[...] = jnp.where(info[X] + d < 4, kv, gr)


def back_kernel(info, g0, g1, g2, g3, c1, c2, c3, o0, o1, o2, o3):
    enter_kv = jnp.zeros((DH, DH), F32)
    enter_gr = jnp.zeros((DH, DH), F32)
    for d, ref in ((1, c1), (2, c2), (3, c3)):
        earlier = info[X] >= d
        enter_kv = enter_kv + jnp.where(earlier, ref[...], 0.0)
        enter_gr = enter_gr + jnp.where(earlier, 0.0, ref[...])
    for e, out in enumerate((o0, o1, o2, o3)):
        there = (info[Y] + e) % 4
        kv, gr = enter_kv, enter_gr
        for d, ref in enumerate((g0, g1, g2, g3)):
            here = (info[Y] + 4 - d) % 4
            kv = kv + jnp.where(here < there, ref[0], 0.0)
            gr = gr + jnp.where(here > there, ref[1], 0.0)
        out[0] = kv
        out[1] = gr


def intra_kernel(pair):
    def kernel(p_ref, g_ref, att_ref, dq_ref, dk_ref, dv_ref):
        rows = lax.broadcasted_iota(jnp.int32, (BLK, BLK), 0)
        cols = lax.broadcasted_iota(jnp.int32, (BLK, BLK), 1)
        causal = rows >= cols
        for i in range(2):
            h = 2 * pair + i
            to = slice(i * DH, i * DH + DH)
            q, k, v = (p_ref[:, head(kind, h)] for kind in range(3))
            g = g_ref[:, head(0, h)]
            scores = jnp.where(causal, dot(q, k, 1, 1), 0.0).astype(BF16)
            att_ref[:, to] = dot(scores, v, 1, 0)
            dv_ref[:, to] = dot(scores, g, 0, 0)
            grad_scores = jnp.where(causal, dot(g, v, 1, 1), 0.0).astype(BF16)
            dq_ref[:, to] = dot(grad_scores, k, 1, 0)
            dk_ref[:, to] = dot(grad_scores, q, 0, 0)

    return kernel


def turn_kernel(own_ref, wide_ref, o_ref):
    for j in range(4):
        at = slice(j * 512, j * 512 + 512)
        o_ref[at, 0:512] = own_ref[:, at].T
        o_ref[at, 512:1024] = wide_ref[:, at].astype(BF16).T


def settle_kernel(info, m0, m1, m2, m3, own_ref, other_ref, o_ref):
    c = info[CORE].astype(F32)
    o_ref[...] = jnp.zeros(o_ref.shape, BF16)
    for j, ref in enumerate((m0, m1, m2, m3)):
        for h in range(NEAR):

            @pl.when((info[Y] + 4 - j) % 4 == h)
            def _():
                at = slice((h % 2) * DH, (h % 2) * DH + DH)
                o_ref[0, h // 2, 0, at, at] = (ref[0] + c * other_ref[h, 0]).astype(BF16)
                o_ref[0, h // 2, 1, at, at] = (ref[1] + (1.0 - c) * other_ref[h, 1]).astype(BF16)
                o_ref[1, h // 2, 0, at, at] = (ref[0] + (1.0 - c) * own_ref[h, 0]).astype(BF16)
                o_ref[1, h // 2, 1, at, at] = (ref[1] + c * own_ref[h, 1]).astype(BF16)


def pair_of(kind, pair):
    return slice(kind * HALF + pair * 256, kind * HALF + pair * 256 + 256)


def rows_of(block):
    return slice(block * BLK, block * BLK + BLK)


def query_kernel(info, st_ref, go_ref, gp_ref, d00, d01, d10, d11, xt_ref, dq_ref, o_ref):
    parts = ((d00, d01), (d10, d11))
    for block, g_ref in enumerate((go_ref, gp_ref)):
        for pair in range(2):
            at = pair_of(0, pair)
            far = dot(g_ref[:, at], st_ref[block, pair, 0], 1, 1)
            dq_ref[rows_of(block), at] = (parts[block][pair][...] + far).astype(BF16)
    partial_x_kernel(0)(info, xt_ref, dq_ref, o_ref)


def key_value_kernel(
    st_ref, po_ref, pp_ref, k00, k01, k10, k11, v00, v01, v10, v11, dq_ref, dk_ref, dv_ref, wide_ref
):
    keys = ((k00, k01), (k10, k11))
    values = ((v00, v01), (v10, v11))
    for block, p_ref in enumerate((po_ref, pp_ref)):
        for pair in range(2):
            at = pair_of(0, pair)
            gr = st_ref[block, pair, 1]
            far = dot(p_ref[:, pair_of(2, pair)], gr, 1, 1)
            dk_ref[rows_of(block), at] = (keys[block][pair][...] + far).astype(BF16)
            far = dot(p_ref[:, pair_of(1, pair)], gr, 1, 0)
            dv_ref[rows_of(block), at] = (values[block][pair][...] + far).astype(BF16)
    for kind, ref in enumerate((dq_ref, dk_ref, dv_ref)):
        wide_ref[kind] = ref[512:1024, :].astype(F32)


def attend_kernel(info, st_ref, po_ref, pp_ref, a00, a01, a10, a11, own_ref, other_ref):
    parts = ((a00, a01), (a10, a11))
    scale = scale_of(info[BASE])
    for block, p_ref in enumerate((po_ref, pp_ref)):
        for pair in range(2):
            at = pair_of(0, pair)
            total = parts[block][pair][...] + dot(p_ref[:, at], st_ref[block, pair, 0], 1, 0)
            if block == 0:
                for i in range(2):
                    to = slice(pair * 256 + i * DH, pair * 256 + i * DH + DH)
                    own_ref[:, to] = (total[:, i * DH : i * DH + DH] * scale).astype(BF16)
            else:
                other_ref[:, at] = total


def attended_kernel(info, own_ref, back_ref, o_ref):
    scale = scale_of(info[BASE])
    for c in range(2):

        @pl.when(info[CORE] == c)
        def _():
            o_ref[:, c * HALF : c * HALF + HALF] = own_ref[...]
            for h in range(NEAR):
                to = slice((1 - c) * HALF + h * DH, (1 - c) * HALF + h * DH + DH)
                o_ref[:, to] = (back_ref[:, head(0, h)] * scale).astype(BF16)


def put(info, o_ref, lead, row, col, value):
    c = info[CORE]
    for i in range(2):
        half = jnp.where(c == i, 1, 0)
        o_ref[(*lead, half)] = value[row + i * 64 : row + i * 64 + 64, col : col + 128]


def slot(info, axis, i):
    return info[SLOTS[axis] + i]


def partial_x_kernel(keep):
    def kernel(info, xt_ref, d_ref, o_ref):
        for g in range(2):
            at = pl.multiple_of(info[PICKS["x"] + 2 * keep + g] * 512, 512)
            total = dot(xt_ref[pl.ds(at, 512), :], d_ref[...], 1, 0)
            for y in range(4):
                for z in range(4):
                    lead = (g, slot(info, "y", y), slot(info, "z", z))
                    put(info, o_ref, lead, y * 128, z * 128, total)

    return kernel


def partial_y_kernel(keep):
    def kernel(info, xt_ref, d_ref, o_ref):
        for g in range(2):
            y = info[PICKS["y"] + 2 * keep + g]
            left = [xt_ref[pl.ds(pl.multiple_of(x * 512 + y * 128, 128), 128), :] for x in range(4)]
            total = dot(jnp.concatenate(left, 0), d_ref[...], 1, 0)
            for x in range(4):
                for z in range(4):
                    lead = (g, slot(info, "z", z), slot(info, "x", x))
                    put(info, o_ref, lead, x * 128, z * 128, total)

    return kernel


def partial_z_kernel(keep):
    def kernel(info, xt_ref, d_ref, o_ref):
        right = []
        for g in range(2):
            at = pl.multiple_of(info[PICKS["z"] + 2 * keep + g] * 128, 128)
            right.append(d_ref[:, pl.ds(at, 128)])
        right = jnp.concatenate(right, 1)
        for x in range(4):
            total = dot(xt_ref[x * 512 : x * 512 + 512, :], right, 1, 0)
            for g in range(2):
                for y in range(4):
                    lead = (g, slot(info, "x", x), slot(info, "y", y))
                    put(info, o_ref, lead, y * 128, g * 128, total)

    return kernel


def tokens_out_kernel(half):
    def kernel(info, dq_ref, dk_ref, dv_ref, back_ref, wo_ref, w_ref, *rest):
        first_ref = rest[0] if half else None
        o_ref, d_ref, wp_ref, sems = rest[half:]

        def copy(j, kind):
            at = pl.multiple_of((2 * kind + 1 - info[CORE]) * HALF, HALF)
            return pltpu.make_async_copy(
                w_ref.at[pl.ds(half * 1024 + j * 512, 512), pl.ds(at, HALF)],
                wp_ref.at[pl.ds(j * 512, 512), pl.ds(kind * HALF, HALF)],
                sems.at[3 * j + kind],
            )

        for j in range(2):
            for kind in range(3):
                copy(j, kind).start()
        for kind, ref in enumerate((dq_ref, dk_ref, dv_ref)):
            at = slice(kind * HALF, kind * HALF + HALF)
            d_ref[0, :, at] = ref[0:512, :]
            d_ref[1, :, at] = back_ref[kind].astype(BF16)
        if half:
            o_ref[:, 0:1024] = first_ref[...]
        for j in range(2):
            at = half * 1024 + j * 512
            own = dot(d_ref[0], wo_ref[at : at + 512, :], 1, 1)
            for kind in range(3):
                copy(j, kind).wait()
            far = dot(d_ref[1], wp_ref[j * 512 : j * 512 + 512, :], 1, 1)
            o_ref[:, at : at + 512] = (own + far).astype(BF16)

    return kernel


def second_kernel(kept_ref, came_ref, sent_ref, keep_ref):
    sent_ref[...] = kept_ref[:, 0:2] + came_ref[:, 0:2]
    keep_ref[...] = kept_ref[:, 2:4] + came_ref[:, 2:4]


def third_kernel(kept_ref, came_ref, sent_ref, keep_ref):
    sent_ref[...] = kept_ref[:, :, 0:2] + came_ref[:, :, 0:2]
    keep_ref[...] = kept_ref[:, :, 2:4] + came_ref[:, :, 2:4]


def sum_kernel(kept_ref, came_ref, o_ref):
    o_ref[...] = kept_ref[...] + came_ref[...]


def merge_kernel(a, b, kc, cc, own_ref, x_ref, y_ref, both_ref):
    for ref, i, j in ((own_ref, 0, 0), (x_ref, 1, 0), (y_ref, 0, 1), (both_ref, 1, 1)):
        for g in range(2):
            ref[0, g] = a[i, j, g]
            ref[1, g] = b[j, g, i]
            ref[2, g] = kc[g, i, j] + cc[g, i, j]


def gathered_kernel(own_ref, x_ref, y_ref, both_ref, o_ref):
    o_ref[...] = own_ref[...] + x_ref[...] + y_ref[...] + both_ref[...]


def rows_out_kernel(sum_ref, came_ref, to_ref, own_ref):
    for third in range(3):
        for g in range(2):
            total = (sum_ref[third, g] + came_ref[third, 1 - g]) * (1.0 / 256.0)
            to_ref[third, g] = total[0]
            own_ref[third, g] = total[1]


def weight_kernel(info, own_ref, core_ref, z_ref, both_ref, o_ref):
    far, across = info[PICKS["z"]], info[PICKS["z"] + 1]
    near = info[PICKS["z"] + 3]
    mine, other = info[CORE], 1 - info[CORE]
    for ref, core, groups in (
        (own_ref, mine, (info[Z], near)),
        (core_ref, other, (info[Z], far)),
        (z_ref, mine, (far, across)),
        (both_ref, other, (near, across)),
    ):
        for g in range(2):
            for third in range(3):
                first = third * 1024 + core * HALF + groups[g] * DH
                o_ref[:, pl.ds(pl.multiple_of(first, DH), DH)] = ref[third, g]


def after(values, done):
    return lax.optimization_barrier((values, done))[0]


def body(tokens, w_qkv, cotangent):
    device = lax.axis_index("seq") * 4 + lax.axis_index("batch")
    info = lax.dynamic_index_in_dim(jnp.asarray(table()), device, 0, keepdims=False)
    own_x = tokens[0]
    square = (2, DH, DH)
    far_p, w_own = call(
        "project_far",
        project_far_kernel,
        info,
        [own_x, w_qkv],
        [((BLK, 3 * HALF), F32), ((D, 3 * HALF), BF16)],
        scratch=[
            pltpu.VMEM((BLK, D), BF16),
            pltpu.VMEM((D, 3 * HALF), BF16),
            pltpu.SemaphoreType.DMA((7,)),
        ],
        stay=(0, 1),
    )
    other_pw = permute(far_p, core_pairs())
    own_g, sent_g = call(
        "grad",
        grad_kernel,
        info,
        [after(cotangent[0], far_p)],
        [((BLK, HALF), BF16), ((BLK, HALF), F32)],
    )
    other_gw = permute(sent_g, core_pairs())
    (own_p,) = call(
        "project", project_kernel, None, [own_x, after(w_own, own_g)], [((BLK, 3 * HALF), BF16)]
    )
    (own_st,) = call("states", states_kernel, None, [own_p, own_g], [((NEAR,) + square, F32)])
    quarter = ((BLK, 256), F32)

    def intra(pair, p, g):
        return call("intra", intra_kernel(pair), None, [p, g], [quarter] * 4)

    own_parts = [intra(0, *after((own_p, own_g), own_st))]
    other_pw, other_gw = after((other_pw, other_gw), own_parts)
    other_p, other_g, other_st, *pay = call(
        "chip_states",
        chip_states_kernel,
        info,
        [other_pw, other_gw, own_st],
        [((BLK, 3 * HALF), BF16), ((BLK, HALF), BF16), ((NEAR,) + square, F32)] + [(square, F32)] * 4,
        scratch=[pltpu.VMEM((NEAR,) + square, F32)],
    )
    got = [pay[0]] + [permute(pay[d], shift_pairs("y", d)) for d in range(1, 4)]
    (own_wide,) = call("widen", widen_kernel, None, [after(own_x, pay)], [((BLK, D), F32)])
    other_wide = permute(own_wide, core_pairs())
    other_parts = [intra(0, *after((other_p, other_g), own_wide))]
    got = after(got, other_parts)
    rows = call("row", row_kernel, info, got, [((DH, DH), F32)] * 3)
    came = [permute(rows[d - 1], shift_pairs("x", d)) for d in range(1, 4)]
    own_parts.append(intra(1, *after((own_p, own_g), rows)))
    came = after(came, own_parts[1])
    back = call("back", back_kernel, info, got + came, [(square, F32)] * 4)
    mine = [back[0]] + [permute(back[e], shift_pairs("y", e)) for e in range(1, 4)]
    other_parts.append(intra(1, *after((other_p, other_g), back)))
    (xt,) = call("turn", turn_kernel, None, after([own_x, other_wide], back), [((D, 1024), BF16)])
    mine = after(mine, (other_parts[1], xt))
    (state,) = call(
        "settle", settle_kernel, info, mine + [own_st, other_st], [((2, 2, 2, 256, 256), BF16)]
    )
    parts = [[own_parts[0][i], own_parts[1][i], other_parts[0][i], other_parts[1][i]] for i in range(4)]
    tall = ((1024, HALF), BF16)
    group = ((2, 4, 4, 2, 64, 128), F32)
    dq, sent_x = call(
        "query", query_kernel, info, [state, own_g, other_g] + parts[1] + [xt], [tall, group]
    )
    came_x = permute(sent_x, halving_pairs("x", 0))
    dk, dv, wide_d = call(
        "key_value",
        key_value_kernel,
        None,
        [state, own_p, other_p] + parts[2] + parts[3] + [dq],
        [tall, tall, ((3, BLK, HALF), F32)],
    )
    back_d = permute(wide_d, core_pairs())
    (sent_y,) = call("partial_y", partial_y_kernel(0), info, [xt, dk], [group])
    came_y = permute(sent_y, halving_pairs("y", 0))
    (sent_z,) = call("partial_z", partial_z_kernel(0), info, [xt, after(dv, sent_y)], [group])
    came_z = permute(sent_z, halving_pairs("z", 0))
    (kept_x,) = call("partial_x", partial_x_kernel(1), info, after([xt, dq], sent_z), [group])
    (kept_y,) = call("partial_y", partial_y_kernel(1), info, after([xt, dk], kept_x), [group])
    (kept_z,) = call("partial_z", partial_z_kernel(1), info, after([xt, dv], kept_y), [group])
    own_att, other_att = call(
        "attend",
        attend_kernel,
        info,
        [after(state, kept_z), own_p, other_p] + parts[0],
        [((BLK, HALF), BF16), ((BLK, HALF), F32)],
    )
    att_back = permute(other_att, core_pairs())
    low = [
        pltpu.VMEM((2, BLK, 3 * HALF), BF16),
        pltpu.VMEM((1024, 3 * HALF), BF16),
        pltpu.SemaphoreType.DMA((6,)),
    ]
    d_args = after([dq, dk, dv, back_d], other_att)
    (token_half,) = call(
        "tokens_out",
        tokens_out_kernel(0),
        info,
        d_args + [w_own, w_qkv],
        [((BLK, 1024), BF16)],
        scratch=low,
        stay=(5,),
    )
    thirds = [["xyz", kept_x, came_x], ["yzx", kept_y, came_y], ["zxy", kept_z, came_z]]
    last = token_half
    for step, kernel, shape in ((1, second_kernel, (2, 2, 4)), (2, third_kernel, (2, 2, 2))):
        for third in thirds:
            axes, kept, came = third
            last, keep = call(
                "halve", kernel, None, [kept, after(came, last)], [(shape + (2, 64, DH), F32)] * 2
            )
            third[1:] = [keep, permute(last, halving_pairs(axes[step], 0))]
        if step == 1:
            (token_grad,) = call(
                "tokens_out",
                tokens_out_kernel(1),
                info,
                after(d_args, last) + [w_own, w_qkv, token_half],
                [((BLK, D), BF16)],
                scratch=low,
                stay=(5,),
            )
            (attended,) = call(
                "attended",
                attended_kernel,
                info,
                [own_att, after(att_back, token_grad)],
                [((BLK, 2 * HALF), BF16)],
            )
            last = attended
    block = ((3, 2, 2, 64, DH), F32)
    small = ((2, 2, 2, 2, 64, DH), F32)
    (sum_a,) = call("sum", sum_kernel, None, thirds[0][1:], [small])
    (sum_b,) = call("sum", sum_kernel, None, [thirds[1][1], after(thirds[1][2], sum_a)], [small])
    mine_w, to_x, to_y, to_both = call(
        "merge",
        merge_kernel,
        None,
        [sum_a, sum_b, thirds[2][1], after(thirds[2][2], sum_b)],
        [block] * 4,
    )
    from_x = permute(to_x, halving_pairs("x", 1))
    from_y = permute(to_y, halving_pairs("y", 1))
    from_both = permute(to_both, halving_pairs("xy", 1))
    (total,) = call("gathered", gathered_kernel, None, [mine_w, from_x, from_y, from_both], [block])
    from_z = permute(total, halving_pairs("z", 1))
    to_other, own_w = call(
        "rows_out", rows_out_kernel, None, [total, from_z], [((3, 2, 64, DH), F32)] * 2
    )
    along = [
        own_w,
        permute(to_other, core_pairs()),
        permute(own_w, halving_pairs("z", 0)),
        permute(to_other, halving_pairs("z", 0, True)),
    ]
    (weight_grad,) = call("weight", weight_kernel, info, along, [((64, 3072), F32)])
    return attended[None], token_grad[None], weight_grad


def solution(mesh):
    return jax.shard_map(
        body,
        mesh=mesh,
        in_specs=(P("batch", "seq", None), P(), P("batch", "seq", None)),
        out_specs=(P("batch", "seq", None), P("batch", "seq", None), P("seq", None)),
        check_vma=False,
    )
```
